1024 devices in a mesh: section: 16 (over z), expert: 64 (over y, x, core).
Axes of the slice: x: 4, y: 8, z: 16, core: 2. Of those that a mesh axis runs over, the one named last changes fastest.
Arguments:
- carried: bfloat16 [16, 12288, 2048], P('section', 'expert'), may hold values from -6 to 6
- norm_gain: float32 [16, 2048], P('section'), may hold values from 0.25 to 1.75
- w_up: bfloat16 [16, 2048, 12288], P('section', None, 'expert'), may hold values from -0.125 to 0.125
- w_down: bfloat16 [16, 12288, 2048], P('section', 'expert'), may hold values from -0.21875 to 0.21875
- routes: int32 [1, 16, 12288, 2], P(None, 'section', 'expert'), may hold values from 0 to 15, all different within a row; in each aligned block of 192 rows (0 to 191, 192 to 383, ..., all dimensions but the last counted through in order) at most 32 rows name the same one
- gate_weights: float32 [1, 16, 12288, 2], P(None, 'section', 'expert'), may hold values from 0.3 to 1
Outputs:
- advanced: bfloat16 [16, 12288, 2048], P('section', 'expert')
The draws below stay inside these ranges and needn't reach their ends.
Inputs may be any that keep to these rules, and one draw needn't show every extreme that they name: `routes`: each token names two different experts. Among the 192 tokens of one device at one step and section, no expert is named more than 32 times, a bound that some block reaches.
All inputs are finite; a program needn't handle non-finite values.
Results may differ from the reference program's by a relative error of at most 0.0052.
Values may be sent and summed in bfloat16 or wider, within the bound.
A program may use at most 32 MiB of HBM per device.

```python
import math
import jax
import jax.numpy as jnp
import numpy as np
from jax import lax

D = 2048
H = 768
TOK_DEV = 192
TICKS = 1
EXPERTS = 16
TOKENS = 12288
CAP = 32
N_SECTION = 16
N_EXPERT = 64


def block_scale(key, extent, shards, low, largest):
    loudness = 1.0
    for dim, blocks in shards:
        heights = jax.random.uniform(jax.random.fold_in(jax.random.fold_in(key, 6), dim), (blocks,), jnp.float32, low / len(shards), largest / len(shards))
        loudness = loudness * jnp.repeat(jnp.exp(heights), extent[dim] // blocks).reshape((-1,) + (1,) * (len(extent) - 1 - dim))
    return loudness


def assign_block(own_key, own, number, rows, count, top, bound, lean):
    ranking = jax.random.permutation(own_key, count)
    packed, ordinary = shares(count, rows * top, bound, lean, True), shares(count, rows * top, bound, lean, False)
    places = jnp.arange(count)

    def named(sizes, rotation):
        used = int((sizes > 0).sum())
        fixed = max(1, used // 4)
        shifted = fixed + (places - fixed + rotation * (used - fixed)) % max(1, count - fixed)
        return jnp.zeros((count,), jnp.int32).at[ranking[jnp.where(places < fixed, places, shifted)]].set(jnp.asarray(sizes, jnp.int32))

    sizes = jnp.where(number % 4 == 0, named(packed, number // 4), named(ordinary, number - number // 4 - 1))
    mixed = jax.random.permutation(jax.random.fold_in(own, 3), count)
    donor, sink = mixed[0:count // 2 * 2:2], mixed[1:count // 2 * 2:2]
    margin = jnp.minimum(sizes[donor] - 1, bound - sizes[sink]) // 2
    margin = jnp.where((donor == ranking[0]) | (sink == ranking[0]) | (sizes[sink] == 0), 0, jnp.maximum(margin, 0))
    shifted = jax.random.randint(jax.random.fold_in(own, 4), (count // 2,), 0, 1 << 20) % (margin + 1)
    sizes = sizes.at[donor].add(-shifted).at[sink].add(shifted)
    labels = jnp.searchsorted(jnp.cumsum(sizes), jnp.arange(rows * top), side="right").astype(jnp.int32)
    table = labels.reshape(top, rows).T
    table = table[jax.random.permutation(jax.random.fold_in(own, 1), rows)]
    rotation = jax.random.randint(jax.random.fold_in(own, 2), (rows, 1), 0, top)
    return jnp.take_along_axis(table, (jnp.arange(top)[None, :] + rotation) % top, axis=1)


def shares(number_of, total, most, lean, full):
    portions = [(1 << 20) // math.isqrt(rank ** lean) + 1 for rank in range(1, number_of + 1)]
    largest = most if full else min(most, max(-(-total // number_of), total * portions[0] // sum(portions)))
    least = 1 if total - largest >= number_of - 1 else 0
    given, rest = [largest] + [least] * (number_of - 1), total - largest - least * (number_of - 1)
    while rest > 0:
        candidates = [i for i in range(1, number_of) if given[i] < largest] or [i for i in range(1, number_of) if given[i] < most]
        whole, remaining = sum([portions[i] for i in candidates]), rest
        for i in candidates:
            addition = min(most - given[i], max(1, remaining * portions[i] // whole), rest)
            given[i] = given[i] + addition
            rest = rest - addition
    return np.array(given)


def scatter_about(key, extent, width, reach, shards=(), kind=jnp.bfloat16):
    entries = jax.random.normal(key, extent, jnp.float32) * width
    if len(shards) > 0:
        entries = block_scale(key, extent, shards, -0.22, 0.18) * entries
    return jnp.clip(entries, min=-reach, max=reach).astype(kind)


def setup_inputs(seed: int = 0) -> dict:
    splits = jax.random.split(jax.random.key(seed), 7)
    carried = scatter_about(splits[0], (N_SECTION, TOKENS, D), 1.0, 6.0, ((0, 16), (1, 64)))
    norm_gain = jnp.clip(1.0 + 0.15 * jax.random.normal(splits[1], (N_SECTION, D), jnp.float32), 0.25, 1.75)
    w_up = scatter_about(splits[2], (N_SECTION, D, EXPERTS * H), D ** -0.5, 0.125, ((0, 16), (2, 64)))
    w_down = scatter_about(splits[3], (N_SECTION, EXPERTS * H, D), H ** -0.5, 0.21875, ((0, 16), (1, 64)))
    routes_keys = jax.random.split(jax.random.fold_in(splits[4], 1), TICKS * N_SECTION * TOKENS // TOK_DEV)
    routes_turns = jax.random.permutation(jax.random.fold_in(splits[4], 3), TICKS * N_SECTION * TOKENS // TOK_DEV)
    routes = jax.vmap(lambda own, number: assign_block(jax.random.fold_in(splits[4], 2), own, number, TOK_DEV, EXPERTS, 2, CAP, 1))(routes_keys, routes_turns).reshape((TICKS, N_SECTION, TOKENS, 2))
    gate_weights = jnp.clip(0.3 + 0.7 * jax.random.uniform(splits[5], (TICKS, N_SECTION, TOKENS, 2), jnp.float32) ** block_scale(splits[5], (TICKS, N_SECTION, TOKENS, 2), ((1, 16), (2, 64)), -0.2, 0.2), 0.3, 1.0)
    return {"carried": carried, "norm_gain": norm_gain, "w_up": w_up, "w_down": w_down, "routes": routes, "gate_weights": gate_weights}


def half_output(row_block, up_part, down_part):
    hidden = jax.nn.gelu(jnp.dot(row_block, up_part, preferred_element_type=jnp.float32)).astype(jnp.bfloat16)
    return jnp.dot(hidden, down_part, preferred_element_type=jnp.float32).astype(jnp.bfloat16)

def section_layer(current, gain_row, up_section, down_section, expert_ids, weights_now):
    experts = N_EXPERT // 4
    capacity = min(TOK_DEV, 4 * ((5 * TOK_DEV + 8 * experts - 1) // (8 * experts)))
    half_width = H // 2
    per_expert = N_EXPERT * capacity
    values = current.astype(jnp.float32)
    inverse_rms = lax.rsqrt(lax.optimization_barrier(jnp.mean(values * values, axis=-1, keepdims=True)) + 1e-05)
    normed = (values * inverse_rms * gain_row).astype(jnp.bfloat16)
    flat_ids = expert_ids.reshape(N_EXPERT, TOK_DEV * 2)
    one_hot = (flat_ids[:, :, None] == jnp.arange(experts, dtype=jnp.int32)[None, None, :]).astype(jnp.int32)
    position = lax.optimization_barrier(jnp.sum((jnp.cumsum(one_hot, axis=1) - one_hot) * one_hot, axis=2))
    sources = jnp.arange(N_EXPERT, dtype=jnp.int32)[:, None]
    slot_keys = (flat_ids * per_expert + sources * capacity + position).reshape(-1).astype(jnp.int32)
    row_ids = jnp.arange(TOKENS * 2, dtype=jnp.int32) // 2
    slot_table = jnp.full((experts * per_expert,), TOKENS, jnp.int32).at[slot_keys].set(row_ids)
    slot_table = slot_table.reshape(experts, per_expert)
    padded = jnp.concatenate([normed, jnp.zeros((1, D), jnp.bfloat16)], axis=0)

    def one_expert(expert):
        row_block = padded[slot_table[expert]]
        total = jnp.zeros((per_expert, D), jnp.float32)
        for half in range(2):
            col_start = (expert * H + half * half_width).astype(jnp.int32)
            up_part = lax.dynamic_slice_in_dim(up_section, col_start, half_width, 1)
            down_part = lax.dynamic_slice_in_dim(down_section, col_start, half_width, 0)
            total = total + half_output(row_block, up_part, down_part).astype(jnp.float32)
        return total.astype(jnp.bfloat16)
    outputs = lax.map(one_expert, jnp.arange(experts, dtype=jnp.int32))
    gathered = outputs.reshape(-1, D)[slot_keys].astype(jnp.float32).reshape(TOKENS, 2, D)
    updated = values + weights_now[:, 0:1] * gathered[:, 0] + weights_now[:, 1:2] * gathered[:, 1]
    return updated.astype(jnp.bfloat16)

def reference(carried, norm_gain, w_up, w_down, routes, gate_weights):
    current = carried
    for tick_index in range(TICKS):

        def per_section(section_index):
            return section_layer(current[section_index], norm_gain[section_index], w_up[section_index], w_down[section_index], routes[tick_index, section_index], gate_weights[tick_index, section_index])
        updated = lax.map(per_section, jnp.arange(N_SECTION, dtype=jnp.int32))
        current = jnp.roll(updated, 1, axis=0)
    return current
```

```python
import jax
import jax.numpy as jnp
from jax import lax
from jax.experimental import pallas as pl
from jax.experimental.pallas import tpu as pltpu
from jax.sharding import PartitionSpec as P

MESH = pl.DeviceIdType.MESH
NX, NY, NC = 4, 8, 2
CHIPS = NX * NY
ROWS = 16
CHUNKS = 4


def kernel(
    x_ref, gain_ref, up_ref, down_ref, routes_ref, gates_ref, out_ref,
    up_all, down_all, normed, send, recv, hidden, res, back, mix, outb,
    own_sem, sib_send, sib_recv, xp_send, xp_recv, fwd_send, fwd_recv,
    self_sem, go_send, go_recv, home_self, home_send, home_recv, out_send, out_recv,
):
    tokens, width = x_ref.shape
    quarter = up_ref.shape[0]
    slots = CHIPS * ROWS
    experts = CHIPS // 2
    cap = 2 * ROWS
    cols = width // CHUNKS
    sections = lax.axis_size("section")
    section = lax.axis_index("section")
    me = lax.axis_index("expert")
    core = lax.rem(me, NC)
    chip = lax.div(me, NC)
    x = lax.rem(chip, NX)
    y = lax.div(chip, NX)

    def away(i, sign):
        k, m = lax.div(i, NX), lax.rem(i, NX)
        dy = NY // 2 + (1 - 2 * lax.rem(k, 2)) * lax.div(k + 1, 2)
        dx = NX // 2 + (1 - 2 * lax.rem(m, 2)) * lax.div(m + 1, 2)
        return lax.rem(y + NY + sign * dy, NY) * NX + lax.rem(x + NX + sign * dx, NX)

    def at(which):
        return (section, which * NC + core)

    sibling = (section, chip * NC + 1 - core)
    beside = (section, (chip + 1 - 2 * lax.rem(x, 2)) * NC + core)
    following = (lax.rem(section + 1, sections), me)
    previous = (lax.rem(section + sections - 1, sections), me)

    barrier = pltpu.get_barrier_semaphore()

    def greet(i, carry):
        pl.semaphore_signal(barrier, inc=1, device_id=at(away(i, 1)), device_id_type=MESH)
        return carry

    lax.fori_loop(0, CHIPS - 1, greet, 0)
    pl.semaphore_signal(barrier, inc=1, device_id=sibling, device_id_type=MESH)
    pl.semaphore_signal(barrier, inc=1, device_id=previous, device_id_type=MESH)

    own_up = pltpu.make_async_copy(up_ref, up_all.at[pl.ds(0, quarter)], own_sem.at[0])
    own_down = pltpu.make_async_copy(down_ref, down_all.at[pl.ds(0, quarter)], own_sem.at[1])
    own_up.start()
    own_down.start()

    block = 48

    def norm(i, carry):
        rows = pl.ds(pl.multiple_of(i * block, 16), block)
        values = x_ref[rows, :].astype(jnp.float32)
        inverse = lax.rsqrt(jnp.mean(values * values, axis=-1, keepdims=True) + 1e-05)
        normed[rows, :] = (values * inverse * gain_ref[...]).astype(jnp.bfloat16)
        return carry

    lax.fori_loop(0, tokens // block, norm, 0)
    pl.semaphore_wait(barrier, CHIPS + 1)

    def remote(src, dst, send_sem, recv_sem, device):
        return pltpu.make_async_remote_copy(
            src_ref=src, dst_ref=dst, send_sem=send_sem, recv_sem=recv_sem,
            device_id=device, device_id_type=MESH,
        )

    beside_copies = [
        remote(own, whole.at[pl.ds(2 * quarter, quarter)], xp_send.at[j], xp_recv.at[j], beside)
        for j, (own, whole) in enumerate(((up_ref, up_all), (down_ref, down_all)))
    ]
    sibling_copies = [
        remote(own, whole.at[pl.ds(quarter, quarter)], sib_send.at[j], sib_recv.at[j], sibling)
        for j, (own, whole) in enumerate(((up_ref, up_all), (down_ref, down_all)))
    ]
    for copy in beside_copies + sibling_copies:
        copy.start()

    ids = routes_ref[...]
    names = lax.broadcasted_iota(jnp.int32, (experts, tokens), 0)
    first = (names == ids[0:1, :]).astype(jnp.float32)
    second = (names == ids[1:2, :]).astype(jnp.float32)
    earlier = (
        lax.broadcasted_iota(jnp.int32, (tokens, tokens), 0)
        < lax.broadcasted_iota(jnp.int32, (tokens, tokens), 1)
    ).astype(jnp.bfloat16)
    count = jnp.dot((first + second).astype(jnp.bfloat16), earlier, preferred_element_type=jnp.float32)
    place0 = jnp.sum(count * first, axis=0, keepdims=True).astype(jnp.int32) + ids[0:1, :] * cap
    place1 = jnp.sum(count * second, axis=0, keepdims=True).astype(jnp.int32) + ids[1:2, :] * cap
    slot = lax.broadcasted_iota(jnp.int32, (slots, tokens), 0)
    is0, is1 = slot == place0, slot == place1
    assign = (is0 | is1).astype(jnp.float32).astype(jnp.bfloat16)

    def fill(i, carry):
        part = pl.ds(pl.multiple_of(i * cols, 128), cols)
        send[:, part] = jnp.dot(
            assign, normed[:, part], preferred_element_type=jnp.float32
        ).astype(jnp.bfloat16)
        return carry

    lax.fori_loop(0, CHUNKS, fill, 0)

    def slots_of(which):
        return pl.ds(pl.multiple_of(which * ROWS, ROWS), ROWS)

    def go(i, carry):
        target = away(i, 1)
        remote(send.at[slots_of(target)], recv.at[slots_of(i)], go_send, go_recv, at(target)).start()
        return carry

    lax.fori_loop(0, CHIPS - 1, go, 0)
    stay = pltpu.make_async_copy(send.at[slots_of(chip)], recv.at[slots_of(CHIPS - 1)], self_sem)
    stay.start()

    gates = gates_ref[...]
    weight = jnp.where(is0, gates[0:1, :], 0.0) + jnp.where(is1, gates[1:2, :], 0.0)
    weight = weight.T
    high = weight.astype(jnp.bfloat16)
    mix[:, pl.ds(0, slots)] = high
    mix[:, pl.ds(slots, slots)] = (weight - high.astype(jnp.float32)).astype(jnp.bfloat16)

    forward_copies = [
        remote(
            whole.at[pl.ds(2 * quarter, quarter)], whole.at[pl.ds(3 * quarter, quarter)],
            fwd_send.at[j], fwd_recv.at[j], sibling,
        )
        for j, whole in enumerate((up_all, down_all))
    ]
    for j in range(2):
        beside_copies[j].wait_recv()
        forward_copies[j].start()
    own_up.wait()
    own_down.wait()
    for j in range(2):
        sibling_copies[j].wait()
    forward_copies[0].wait_recv()
    stay.wait()
    everyone = pl.ds(0, slots - ROWS)
    went = remote(send.at[everyone], recv.at[everyone], go_send, go_recv, sibling)
    went.wait_recv()

    units = 256

    def up(i, carry):
        part = pl.ds(pl.multiple_of(i * units, units), units)
        v = lax.dot_general(
            recv[...], up_all[part, :], (((1,), (1,)), ((), ())), preferred_element_type=jnp.float32
        )
        inner = 0.7978845608028654 * (v + 0.044715 * (v * v * v))
        hidden[:, part] = (0.5 * v * (1.0 + jnp.tanh(inner))).astype(jnp.bfloat16)
        return carry

    lax.fori_loop(0, 4 * quarter // units, up, 0)
    forward_copies[1].wait_recv()

    def down(c, carry):
        part = pl.ds(pl.multiple_of(c * cols, 128), cols)
        res[c] = jnp.dot(
            hidden[...], down_all[:, part], preferred_element_type=jnp.float32
        ).astype(jnp.bfloat16)

        def home(i, inner):
            target = away(i, -1)
            remote(
                res.at[c, slots_of(i)], back.at[c, slots_of(chip)],
                home_send.at[c], home_recv.at[c], at(target),
            ).start()
            return inner

        lax.fori_loop(0, CHIPS - 1, home, 0)
        pltpu.make_async_copy(
            res.at[c, slots_of(CHIPS - 1)], back.at[c, slots_of(chip)], home_self.at[c]
        ).start()
        return carry

    lax.fori_loop(0, CHUNKS, down, 0)

    def onward(c):
        part = pl.ds(pl.multiple_of(c * cols, 128), cols)
        return remote(outb.at[c], out_ref.at[:, part], out_send.at[c], out_recv.at[c], following)

    def came_home(c):
        return remote(res.at[c, everyone], back.at[c, everyone], home_send.at[c], home_recv.at[c], sibling)

    def finish(c, carry):
        part = pl.ds(pl.multiple_of(c * cols, 128), cols)
        pltpu.make_async_copy(
            res.at[c, slots_of(CHIPS - 1)], back.at[c, slots_of(chip)], home_self.at[c]
        ).wait()
        came_home(c).wait_recv()
        rows = back[c]
        total = jnp.dot(mix[:, pl.ds(0, slots)], rows, preferred_element_type=jnp.float32)
        total += jnp.dot(mix[:, pl.ds(slots, slots)], rows, preferred_element_type=jnp.float32)
        outb[c] = (x_ref[:, part].astype(jnp.float32) + total).astype(jnp.bfloat16)
        onward(c).start()
        return carry

    lax.fori_loop(0, CHUNKS, finish, 0)

    for j in range(2):
        beside_copies[j].wait_send()
        forward_copies[j].wait_send()
    went.wait_send()

    def drain(c, carry):
        came_home(c).wait_send()
        onward(c).wait()
        return carry

    lax.fori_loop(0, CHUNKS, drain, 0)


def shards(carried, norm_gain, w_up, w_down, routes, gate_weights):
    tokens, width = carried.shape[1:]
    quarter = w_down.shape[1]
    slots = CHIPS * ROWS
    cols = width // CHUNKS
    bf16 = jnp.bfloat16
    dma = pltpu.SemaphoreType.DMA
    vmem = pl.BlockSpec(memory_space=pltpu.VMEM)
    whole = pl.BlockSpec(memory_space=pl.ANY)
    out = pl.pallas_call(
        kernel,
        name="section_layer",
        out_shape=jax.ShapeDtypeStruct((tokens, width), bf16),
        in_specs=[vmem, vmem, whole, whole, vmem, vmem],
        out_specs=whole,
        scratch_shapes=[
            pltpu.VMEM((4 * quarter, width), bf16),
            pltpu.VMEM((4 * quarter, width), bf16),
            pltpu.VMEM((tokens, width), bf16),
            pltpu.VMEM((slots, width), bf16),
            pltpu.VMEM((slots, width), bf16),
            pltpu.VMEM((slots, 4 * quarter), bf16),
            pltpu.VMEM((CHUNKS, slots, cols), bf16),
            pltpu.VMEM((CHUNKS, slots, cols), bf16),
            pltpu.VMEM((tokens, 2 * slots), bf16),
            pltpu.VMEM((CHUNKS, tokens, cols), bf16),
            dma((2,)), dma((2,)), dma((2,)), dma((2,)), dma((2,)), dma((2,)), dma((2,)),
            dma, dma, dma,
            dma((CHUNKS,)), dma((CHUNKS,)), dma((CHUNKS,)), dma((CHUNKS,)), dma((CHUNKS,)),
        ],
        compiler_params=pltpu.CompilerParams(
            collective_id=0, has_side_effects=True, vmem_limit_bytes=52 * 1024 * 1024
        ),
        cost_estimate=pl.CostEstimate(
            flops=8 * slots * width * quarter * 2, bytes_accessed=4 * quarter * width * 2, transcendentals=0
        ),
    )(carried[0], norm_gain, w_up[0].T, w_down[0], routes[0, 0].T, gate_weights[0, 0].T)
    return out[None]


def solution(mesh):
    in_specs = (
        P("section", "expert", None),
        P("section", None),
        P("section", None, "expert"),
        P("section", "expert", None),
        P(None, "section", "expert", None),
        P(None, "section", "expert", None),
    )
    return jax.shard_map(
        shards, mesh=mesh, in_specs=in_specs, out_specs=P("section", "expert", None), check_vma=False
    )
```

```python
import jax
import jax.numpy as jnp
from jax import lax
from jax.experimental import pallas as pl
from jax.experimental.pallas import tpu as pltpu
from jax.sharding import PartitionSpec as P

MESH = pl.DeviceIdType.MESH
NX, NY, NC = 4, 8, 2
PEERS = 2 * NY
EXPERTS = NX * NY // 2
GROUPS = ((0, 10), (10, 16))
WIDTHS = (640, 640, 512, 256)
STARTS = tuple(sum(WIDTHS[:c]) for c in range(len(WIDTHS)))


def kernel(
    x_hbm, gain_hbm, up_ref, down_ref, routes_hbm, gates_hbm, out_ref,
    x_ref, gain_ref, routes_ref, gates_ref,
    up_all, down_all, normed, send, recv, hidden, mix, *rest,
):
    chunks = len(WIDTHS)
    res, back, outb = rest[:chunks], rest[chunks : 2 * chunks], rest[2 * chunks : 3 * chunks]
    (
        in_sem, own_sem, sib_send, sib_recv, xp_send, xp_recv, fwd_send, fwd_recv,
        self_sem, go_send, go_recv, home_self, home_send, home_recv, out_send, out_recv,
    ) = rest[3 * chunks :]
    tokens, width = x_ref.shape
    quarter = up_ref.shape[0]
    slots = send.shape[0]
    cap = slots // EXPERTS
    sections = lax.axis_size("section")
    section = lax.axis_index("section")
    me = lax.axis_index("expert")
    core = lax.rem(me, NC)
    chip = lax.div(me, NC)
    x = lax.rem(chip, NX)
    y = lax.div(chip, NX)
    mine = y * 2 + lax.div(x, 2)

    def peer(i, sign):
        k = lax.div(i, 2)
        half = lax.div(k + 1, 2)
        dy = half * (2 * lax.rem(k, 2) - 1)
        return lax.rem(y + NY + sign * dy, NY), lax.rem(i, 2) * (NX - 1 - 2 * x) + x

    def device(py, px):
        return (section, (py * NX + px) * NC + core)

    sibling = (section, chip * NC + 1 - core)
    beside = (section, (chip + 1 - 2 * lax.rem(x, 2)) * NC + core)
    following = (lax.rem(section + 1, sections), me)
    previous = (lax.rem(section + sections - 1, sections), me)

    def hello(target):
        pl.semaphore_signal(barrier, inc=1, device_id=target, device_id_type=MESH)

    barrier = pltpu.get_barrier_semaphore()
    inputs = [
        pltpu.make_async_copy(src, dst, in_sem.at[j])
        for j, (src, dst) in enumerate(
            ((routes_hbm, routes_ref), (gain_hbm, gain_ref), (x_hbm, x_ref), (gates_hbm, gates_ref))
        )
    ]
    for copy in inputs:
        copy.start()

    def greet(i, carry):
        hello(device(*peer(i, -1)))
        return carry

    lax.fori_loop(1, PEERS, greet, 0)
    hello(sibling)
    hello(beside)
    hello(previous)

    own = [
        pltpu.make_async_copy(src, dst.at[pl.ds(0, quarter)], own_sem.at[j])
        for j, (src, dst) in enumerate(((up_ref, up_all), (down_ref, down_all)))
    ]
    for copy in own:
        copy.start()

    inputs[0].wait()
    ids = routes_ref[...]
    names = lax.broadcasted_iota(jnp.int32, (EXPERTS, tokens), 0)
    first = (names == ids[0:1, :]).astype(jnp.float32)
    second = (names == ids[1:2, :]).astype(jnp.float32)
    earlier = (
        lax.broadcasted_iota(jnp.int32, (tokens, tokens), 0)
        < lax.broadcasted_iota(jnp.int32, (tokens, tokens), 1)
    ).astype(jnp.bfloat16)
    count = jnp.dot((first + second).astype(jnp.bfloat16), earlier, preferred_element_type=jnp.float32)
    place0 = jnp.sum(count * first, axis=0, keepdims=True).astype(jnp.int32) + ids[0:1, :] * cap
    place1 = jnp.sum(count * second, axis=0, keepdims=True).astype(jnp.int32) + ids[1:2, :] * cap
    slot = lax.broadcasted_iota(jnp.int32, (slots, tokens), 0)
    is0, is1 = slot == place0, slot == place1
    assign = (is0 | is1).astype(jnp.float32).astype(jnp.bfloat16)

    block = 48

    def norm(i, carry):
        rows = pl.ds(pl.multiple_of(i * block, 16), block)
        values = x_ref[rows, :].astype(jnp.float32)
        inverse = lax.rsqrt(jnp.mean(values * values, axis=-1, keepdims=True) + 1e-05)
        normed[rows, :] = (values * inverse * gain_ref[...]).astype(jnp.bfloat16)
        return carry

    inputs[1].wait()
    inputs[2].wait()
    with jax.named_scope("p_norm"):
        lax.fori_loop(0, tokens // block, norm, 0)

    piece = 512

    def fill(i, carry):
        part = pl.ds(pl.multiple_of(i * piece, piece), piece)
        send[:, part] = jnp.dot(
            assign, normed[:, part], preferred_element_type=jnp.float32
        ).astype(jnp.bfloat16)
        return carry

    with jax.named_scope("p_fill"):
        lax.fori_loop(0, width // piece, fill, 0)

    with jax.named_scope("p_barrier"):
        pl.semaphore_wait(barrier, PEERS + 2)

    def remote(src, dst, send_sem, recv_sem, target):
        return pltpu.make_async_remote_copy(
            src_ref=src, dst_ref=dst, send_sem=send_sem, recv_sem=recv_sem,
            device_id=target, device_id_type=MESH,
        )

    def rows_of(which):
        return pl.ds(pl.multiple_of(which * cap, cap), cap)

    def group_rows(g, skip=0):
        low, high = GROUPS[g]
        return pl.ds((low + skip) * cap, (high - low - skip) * cap)

    weights = ((up_ref, up_all), (down_ref, down_all))
    beside_copies = [
        remote(src, dst.at[pl.ds(2 * quarter, quarter)], xp_send.at[j], xp_recv.at[j], beside)
        for j, (src, dst) in enumerate(weights)
    ]
    sibling_copies = [
        remote(src, dst.at[pl.ds(quarter, quarter)], sib_send.at[j], sib_recv.at[j], sibling)
        for j, (src, dst) in enumerate(weights)
    ]
    for copy in beside_copies:
        copy.start()

    for g, (low, high) in enumerate(GROUPS):

        def go(i, carry, g=g):
            py, px = peer(i, 1)
            remote(
                send.at[rows_of(py * 2 + lax.div(px, 2))], recv.at[rows_of(i)],
                go_send.at[g], go_recv.at[g], device(py, px),
            ).start()
            return carry

        lax.fori_loop(max(low, 1), high, go, 0)
    stay = pltpu.make_async_copy(send.at[rows_of(mine)], recv.at[rows_of(0)], self_sem)
    stay.start()
    for copy in sibling_copies:
        copy.start()

    inputs[3].wait()
    gates = gates_ref[...]
    weight = jnp.where(is0, gates[0:1, :], 0.0) + jnp.where(is1, gates[1:2, :], 0.0)
    weight = weight.T
    high_part = weight.astype(jnp.bfloat16)
    mix[:, pl.ds(0, slots)] = high_part
    mix[:, pl.ds(slots, slots)] = (weight - high_part.astype(jnp.float32)).astype(jnp.bfloat16)

    forward_copies = [
        remote(
            dst.at[pl.ds(2 * quarter, quarter)], dst.at[pl.ds(3 * quarter, quarter)],
            fwd_send.at[j], fwd_recv.at[j], sibling,
        )
        for j, (_, dst) in enumerate(weights)
    ]
    for copy in own:
        copy.wait()
    for copy in sibling_copies:
        copy.wait()
    stay.wait()

    def went(g):
        rows = group_rows(g, 1 if g == 0 else 0)
        return remote(send.at[rows], recv.at[rows], go_send.at[g], go_recv.at[g], sibling)

    def home_copy(c, g):
        rows = group_rows(g, 1 if g == 0 else 0)
        return remote(res[c].at[rows], back[c].at[rows], home_send.at[c, g], home_recv.at[c, g], sibling)

    def keep(c):
        return pltpu.make_async_copy(res[c].at[rows_of(0)], back[c].at[rows_of(mine)], home_self.at[c])

    for j in range(2):
        with jax.named_scope(f"p_beside{j}"):
            beside_copies[j].wait_recv()
            forward_copies[j].start()
    units = 256
    for g, (low, high) in enumerate(GROUPS):
        rows = group_rows(g)
        with jax.named_scope("p_arrive"):
            went(g).wait_recv()
        if g == 0:
            with jax.named_scope("p_fwd0"):
                forward_copies[0].wait_recv()

        def up(i, carry, rows=rows):
            part = pl.ds(pl.multiple_of(i * units, units), units)
            v = lax.dot_general(
                recv[rows, :], up_all[part, :], (((1,), (1,)), ((), ())),
                preferred_element_type=jnp.float32,
            )
            inner = 0.7978845608028654 * (v + 0.044715 * (v * v * v))
            hidden[rows, part] = (0.5 * v * (1.0 + jnp.tanh(inner))).astype(jnp.bfloat16)
            return carry

        with jax.named_scope("p_up"):
            lax.fori_loop(0, 4 * quarter // units, up, 0)
        if g == 0:
            with jax.named_scope("p_fwd1"):
                forward_copies[1].wait_recv()
        for c in range(chunks):
            with jax.named_scope("p_down"):
                res[c][rows, :] = jnp.dot(
                    hidden[rows, :], down_all[:, pl.ds(STARTS[c], WIDTHS[c])],
                    preferred_element_type=jnp.float32,
                ).astype(jnp.bfloat16)

            def home(i, carry, c=c, g=g):
                py, px = peer(i, -1)
                remote(
                    res[c].at[rows_of(i)], back[c].at[rows_of(mine)],
                    home_send.at[c, g], home_recv.at[c, g], device(py, px),
                ).start()
                return carry

            with jax.named_scope("p_home"):
                lax.fori_loop(max(low, 1), high, home, 0)
            if g == 0:
                keep(c).start()

    onward = [
        remote(
            outb[c], out_ref.at[:, pl.ds(STARTS[c], WIDTHS[c])], out_send.at[c], out_recv.at[c], following
        )
        for c in range(chunks)
    ]
    for c in range(chunks):
        with jax.named_scope("p_came"):
            keep(c).wait()
            for g in range(len(GROUPS)):
                home_copy(c, g).wait_recv()
        with jax.named_scope("p_mix"):
            rows = back[c][...]
            total = jnp.dot(mix[:, pl.ds(0, slots)], rows, preferred_element_type=jnp.float32)
            total += jnp.dot(mix[:, pl.ds(slots, slots)], rows, preferred_element_type=jnp.float32)
            part = pl.ds(STARTS[c], WIDTHS[c])
            outb[c][...] = (x_ref[:, part].astype(jnp.float32) + total).astype(jnp.bfloat16)
            onward[c].start()

    for j in range(2):
        beside_copies[j].wait_send()
        forward_copies[j].wait_send()
    with jax.named_scope("p_drain"):
        for g in range(len(GROUPS)):
            went(g).wait_send()
            for c in range(chunks):
                home_copy(c, g).wait_send()
        for c in range(chunks):
            onward[c].wait()


def shards(carried, norm_gain, w_up, w_down, routes, gate_weights):
    tokens, width = carried.shape[1:]
    quarter = w_down.shape[1]
    slots = EXPERTS * 32
    bf16 = jnp.bfloat16
    dma = pltpu.SemaphoreType.DMA
    whole = pl.BlockSpec(memory_space=pl.ANY)
    chunks = len(WIDTHS)
    out = pl.pallas_call(
        kernel,
        name="section_layer",
        out_shape=jax.ShapeDtypeStruct((tokens, width), bf16),
        in_specs=[whole] * 6,
        out_specs=whole,
        scratch_shapes=[
            pltpu.VMEM((tokens, width), bf16),
            pltpu.VMEM((1, width), jnp.float32),
            pltpu.VMEM((2, tokens), jnp.int32),
            pltpu.VMEM((2, tokens), jnp.float32),
            pltpu.VMEM((4 * quarter, width), bf16),
            pltpu.VMEM((4 * quarter, width), bf16),
            pltpu.VMEM((tokens, width), bf16),
            pltpu.VMEM((slots, width), bf16),
            pltpu.VMEM((slots, width), bf16),
            pltpu.VMEM((slots, 4 * quarter), bf16),
            pltpu.VMEM((tokens, 2 * slots), bf16),
            *[pltpu.VMEM((slots, w), bf16) for w in WIDTHS],
            *[pltpu.VMEM((slots, w), bf16) for w in WIDTHS],
            *[pltpu.VMEM((tokens, w), bf16) for w in WIDTHS],
            dma((4,)), dma((2,)), dma((2,)), dma((2,)), dma((2,)), dma((2,)), dma((2,)), dma((2,)),
            dma, dma((len(GROUPS),)), dma((len(GROUPS),)),
            dma((chunks,)), dma((chunks, len(GROUPS))), dma((chunks, len(GROUPS))),
            dma((chunks,)), dma((chunks,)),
        ],
        compiler_params=pltpu.CompilerParams(
            collective_id=0, has_side_effects=True, vmem_limit_bytes=56 * 1024 * 1024
        ),
        cost_estimate=pl.CostEstimate(
            flops=16 * slots * width * quarter, bytes_accessed=8 * quarter * width, transcendentals=0
        ),
    )(carried[0], norm_gain, w_up[0].T, w_down[0], routes[0, 0].T, gate_weights[0, 0].T)
    return out[None]


def solution(mesh):
    in_specs = (
        P("section", "expert", None),
        P("section", None),
        P("section", None, "expert"),
        P("section", "expert", None),
        P(None, "section", "expert", None),
        P(None, "section", "expert", None),
    )
    return jax.shard_map(
        shards, mesh=mesh, in_specs=in_specs, out_specs=P("section", "expert", None), check_vma=False
    )
```

```python
import jax
import jax.numpy as jnp
from jax import lax
from jax.experimental import pallas as pl
from jax.experimental.pallas import tpu as pltpu
from jax.sharding import PartitionSpec as P

MESH = pl.DeviceIdType.MESH
NX, NY, NC = 4, 8, 2
PEERS = 2 * NY
EXPERTS = NX * NY // 2
GROUPS = ((0, 10), (10, 16))
WIDTHS = (512, 512, 384)
UNITS, UNIT = 5, 128
DIRECT = 5
STARTS = tuple(sum(WIDTHS[:c]) for c in range(len(WIDTHS)))


def kernel(
    x_hbm, gain_hbm, up_ref, down_ref, routes_hbm, gates_hbm, out_ref,
    x_ref, gain_ref, routes_ref, gates_ref,
    up_all, down_all, normed, send, recv, hidden, mix,
    x_far, routes_far, gates_far, mix_far, res_unit, back_unit, out_unit, *rest,
):
    chunks = len(WIDTHS)
    res, back, outb = rest[:chunks], rest[chunks : 2 * chunks], rest[2 * chunks : 3 * chunks]
    (
        in_sem, own_sem, sib_send, sib_recv, xp_send, xp_recv, fwd_send, fwd_recv,
        self_sem, go_send, go_recv, home_self, home_send, home_recv, out_send, out_recv,
        far_send, far_recv, unit_self, unit_send, unit_recv, unit_near, unit_far, unit_out_send, unit_out_recv, far_out, ready, late_ready,
    ) = rest[3 * chunks :]
    tokens, width = x_ref.shape
    quarter = up_ref.shape[0]
    slots = send.shape[0]
    cap = slots // EXPERTS
    sections = lax.axis_size("section")
    section = lax.axis_index("section")
    me = lax.axis_index("expert")
    core = lax.rem(me, NC)
    chip = lax.div(me, NC)
    x = lax.rem(chip, NX)
    y = lax.div(chip, NX)
    mine = y * 2 + lax.div(x, 2)

    def peer(i, sign):
        k = lax.div(i, 2)
        half = lax.div(k + 1, 2)
        dy = half * (2 * lax.rem(k, 2) - 1)
        return lax.rem(y + NY + sign * dy, NY), lax.rem(i, 2) * (NX - 1 - 2 * x) + x

    def device(py, px, where=section):
        return (where, (py * NX + px) * NC + core)

    sibling = (section, chip * NC + 1 - core)
    beside = (section, (chip + 1 - 2 * lax.rem(x, 2)) * NC + core)
    following = (lax.rem(section + 1, sections), me)
    previous = (lax.rem(section + sections - 1, sections), me)
    begin = STARTS[-1] + WIDTHS[-1]
    passed = UNITS - lax.max(0, DIRECT - lax.rem(section + 1, sections))
    taken = UNITS - lax.max(0, DIRECT - section)

    last = sections - 1
    kin = (core == 0) & ((x == 0) | (x == NX - 1))
    is_late = (section == 0) & (me == 0)
    near_late = (section == 0) & (me != 0) & (kin | (me == 1) | (me == NC))
    next_late = (section == 1) & jnp.where(taken < UNITS, kin, me == 0)
    punctual = jnp.logical_not(is_late)
    onward_count = jnp.where(passed < UNITS, PEERS, 1)
    before_count = jnp.where(taken < UNITS, PEERS, 1)

    def hello(target):
        pl.semaphore_signal(barrier, inc=1, device_id=target, device_id_type=MESH)

    barrier = pltpu.get_barrier_semaphore()
    inputs = [
        pltpu.make_async_copy(src, dst, in_sem.at[j])
        for j, (src, dst) in enumerate(
            ((routes_hbm, routes_ref), (gain_hbm, gain_ref), (x_hbm, x_ref), (gates_hbm, gates_ref))
        )
    ]
    for copy in inputs:
        copy.start()

    def greet(i, carry):
        hello(device(*peer(i, -1)))
        return carry

    def greet_at(where, number):
        def greet_far(i, carry):
            hello(device(*peer(i, -1), where))
            return carry

        lax.fori_loop(0, number, greet_far, 0)

    @pl.when(punctual)
    def _():
        lax.fori_loop(1, PEERS, greet, 0)
        hello(sibling)
        hello(beside)

    @pl.when(punctual & (section < last))
    def _():
        greet_at(section + 1, onward_count)

    @pl.when(section == 0)
    def _():
        greet_at(last, before_count)

    @pl.when(next_late)
    def _():
        hello((0, 0))

    own = [
        pltpu.make_async_copy(src, dst.at[pl.ds(0, quarter)], own_sem.at[j])
        for j, (src, dst) in enumerate(((up_ref, up_all), (down_ref, down_all)))
    ]
    for copy in own:
        copy.start()

    def places(ids):
        names = lax.broadcasted_iota(jnp.int32, (EXPERTS, tokens), 0)
        first = (names == ids[0:1, :]).astype(jnp.float32)
        second = (names == ids[1:2, :]).astype(jnp.float32)
        earlier = (
            lax.broadcasted_iota(jnp.int32, (tokens, tokens), 0)
            < lax.broadcasted_iota(jnp.int32, (tokens, tokens), 1)
        ).astype(jnp.bfloat16)
        count = jnp.dot(
            (first + second).astype(jnp.bfloat16), earlier, preferred_element_type=jnp.float32
        )
        place0 = jnp.sum(count * first, axis=0, keepdims=True).astype(jnp.int32) + ids[0:1, :] * cap
        place1 = jnp.sum(count * second, axis=0, keepdims=True).astype(jnp.int32) + ids[1:2, :] * cap
        slot = lax.broadcasted_iota(jnp.int32, (slots, tokens), 0)
        return slot == place0, slot == place1

    def fill_mix(mix, is0, is1, gates):
        weight = jnp.where(is0, gates[0:1, :], 0.0) + jnp.where(is1, gates[1:2, :], 0.0)
        weight = weight.T
        high_part = weight.astype(jnp.bfloat16)
        mix[:, pl.ds(0, slots)] = high_part
        mix[:, pl.ds(slots, slots)] = (weight - high_part.astype(jnp.float32)).astype(jnp.bfloat16)

    def mixed(mix, rows):
        total = jnp.dot(mix[:, pl.ds(0, slots)], rows, preferred_element_type=jnp.float32)
        return total + jnp.dot(mix[:, pl.ds(slots, slots)], rows, preferred_element_type=jnp.float32)

    inputs[0].wait()
    is0, is1 = places(routes_ref[...])
    assign = (is0 | is1).astype(jnp.float32).astype(jnp.bfloat16)

    block = 48

    def norm(i, carry):
        rows = pl.ds(pl.multiple_of(i * block, 16), block)
        values = x_ref[rows, :].astype(jnp.float32)
        inverse = lax.rsqrt(jnp.mean(values * values, axis=-1, keepdims=True) + 1e-05)
        normed[rows, :] = (values * inverse * gain_ref[...]).astype(jnp.bfloat16)
        return carry

    inputs[1].wait()
    inputs[2].wait()
    with jax.named_scope("p_norm"):
        lax.fori_loop(0, tokens // block, norm, 0)

    piece = 512

    def fill(i, carry):
        part = pl.ds(pl.multiple_of(i * piece, piece), piece)
        send[:, part] = jnp.dot(
            assign, normed[:, part], preferred_element_type=jnp.float32
        ).astype(jnp.bfloat16)
        return carry

    with jax.named_scope("p_fill"):
        lax.fori_loop(0, width // piece, fill, 0)

    with jax.named_scope("p_barrier"):
        pl.semaphore_wait(
            barrier,
            PEERS + 1
            - near_late.astype(jnp.int32)
            + jnp.where(section > 0, before_count, 0)
            - next_late.astype(jnp.int32)
            + jnp.where((section == last) | is_late, onward_count, 0),
        )

    def remote(src, dst, send_sem, recv_sem, target):
        return pltpu.make_async_remote_copy(
            src_ref=src, dst_ref=dst, send_sem=send_sem, recv_sem=recv_sem,
            device_id=target, device_id_type=MESH,
        )

    def rows_of(which):
        return pl.ds(pl.multiple_of(which * cap, cap), cap)

    def group_rows(g, skip=0):
        low, high = GROUPS[g]
        return pl.ds((low + skip) * cap, (high - low - skip) * cap)

    weights = ((up_ref, up_all), (down_ref, down_all))
    beside_copies = [
        remote(src, dst.at[pl.ds(2 * quarter, quarter)], xp_send.at[j], xp_recv.at[j], beside)
        for j, (src, dst) in enumerate(weights)
    ]
    sibling_copies = [
        remote(src, dst.at[pl.ds(quarter, quarter)], sib_send.at[j], sib_recv.at[j], sibling)
        for j, (src, dst) in enumerate(weights)
    ]
    @pl.when(is_late)
    def _():
        def arrived(target):
            pl.semaphore_signal(late_ready, inc=1, device_id=target, device_id_type=MESH)

        def tell_peer(i, carry):
            arrived(device(*peer(i, 1)))
            return carry

        lax.fori_loop(1, PEERS, tell_peer, 0)
        arrived(sibling)
        arrived(beside)

    def launch(copies, here):
        @pl.when(here)
        def _():
            for copy in copies:
                copy.start()

    def go_all(late):
        for g, (low, high) in enumerate(GROUPS):

            def go(i, carry, g=g):
                py, px = peer(i, 1)
                target = device(py, px)
                to_late = (section == 0) & (target[1] == 0)

                @pl.when(to_late if late else jnp.logical_not(to_late))
                def _():
                    remote(
                        send.at[rows_of(py * 2 + lax.div(px, 2))], recv.at[rows_of(i)],
                        go_send.at[g], go_recv.at[g], target,
                    ).start()

                return carry

            lax.fori_loop(max(low, 1), high, go, 0)

    beside_late = (section == 0) & (me == NC)
    sibling_late = (section == 0) & (me == 1)
    launch(beside_copies, jnp.logical_not(beside_late))
    go_all(False)
    stay = pltpu.make_async_copy(send.at[rows_of(mine)], recv.at[rows_of(0)], self_sem)
    stay.start()

    @pl.when(section > 0)
    def _():
        def tell(i, carry):
            target = device(*peer(i, 1), section - 1)

            @pl.when(jnp.logical_not((section == 1) & (target[1] == 0)))
            def _():
                pl.semaphore_signal(ready, inc=1, device_id=target, device_id_type=MESH)

            return carry

        lax.fori_loop(0, before_count, tell, 0)

    launch(sibling_copies, jnp.logical_not(sibling_late))
    inputs[3].wait()
    far_copies = [
        remote(src, dst, far_send.at[j], far_recv.at[j], following)
        for j, (src, dst) in enumerate(
            (
                (routes_ref, routes_far),
                (gates_ref, gates_far),
                (x_ref.at[:, pl.ds(begin, UNITS * UNIT)], x_far),
            )
        )
    ]

    fill_mix(mix, is0, is1, gates_ref[...])

    @pl.when(punctual & (section < last))
    def _():
        pl.semaphore_wait(ready, onward_count)

    @pl.when(passed < UNITS)
    def _():
        for copy in far_copies:
            copy.start()

    @pl.when(near_late)
    def _():
        pl.semaphore_wait(late_ready, 1)

    @pl.when(near_late & kin)
    def _():
        go_all(True)

    launch(beside_copies, beside_late)
    launch(sibling_copies, sibling_late)

    forward_copies = [
        remote(
            dst.at[pl.ds(2 * quarter, quarter)], dst.at[pl.ds(3 * quarter, quarter)],
            fwd_send.at[j], fwd_recv.at[j], sibling,
        )
        for j, (_, dst) in enumerate(weights)
    ]
    for copy in own:
        copy.wait()
    for copy in sibling_copies:
        copy.wait()
    stay.wait()

    def went(g):
        rows = group_rows(g, 1 if g == 0 else 0)
        return remote(send.at[rows], recv.at[rows], go_send.at[g], go_recv.at[g], sibling)

    def home_copy(c, g):
        rows = group_rows(g, 1 if g == 0 else 0)
        return remote(res[c].at[rows], back[c].at[rows], home_send.at[c, g], home_recv.at[c, g], sibling)

    def keep(c):
        return pltpu.make_async_copy(res[c].at[rows_of(0)], back[c].at[rows_of(mine)], home_self.at[c])

    for j in range(2):
        with jax.named_scope(f"p_beside{j}"):
            beside_copies[j].wait_recv()
            forward_copies[j].start()
    units = 256
    for g, (low, high) in enumerate(GROUPS):
        rows = group_rows(g)
        with jax.named_scope("p_arrive"):
            went(g).wait_recv()
        if g == 0:
            with jax.named_scope("p_fwd0"):
                forward_copies[0].wait_recv()

        def up(i, carry, rows=rows):
            part = pl.ds(pl.multiple_of(i * units, units), units)
            v = lax.dot_general(
                recv[rows, :], up_all[part, :], (((1,), (1,)), ((), ())),
                preferred_element_type=jnp.float32,
            )
            inner = 0.7978845608028654 * (v + 0.044715 * (v * v * v))
            hidden[rows, part] = (0.5 * v * (1.0 + jnp.tanh(inner))).astype(jnp.bfloat16)
            return carry

        with jax.named_scope("p_up"):
            lax.fori_loop(0, 4 * quarter // units, up, 0)
        if g == 0:
            with jax.named_scope("p_fwd1"):
                forward_copies[1].wait_recv()
        for c in range(chunks):
            with jax.named_scope("p_down"):
                res[c][rows, :] = jnp.dot(
                    hidden[rows, :], down_all[:, pl.ds(STARTS[c], WIDTHS[c])],
                    preferred_element_type=jnp.float32,
                ).astype(jnp.bfloat16)

            def home(i, carry, c=c, g=g):
                py, px = peer(i, -1)
                remote(
                    res[c].at[rows_of(i)], back[c].at[rows_of(mine)],
                    home_send.at[c, g], home_recv.at[c, g], device(py, px),
                ).start()
                return carry

            with jax.named_scope("p_home"):
                lax.fori_loop(max(low, 1), high, home, 0)
            if g == 0:
                keep(c).start()
        tail = jnp.dot(
            hidden[rows, :], down_all[:, pl.ds(begin, UNITS * UNIT)], preferred_element_type=jnp.float32
        ).astype(jnp.bfloat16)
        for j in range(UNITS):
            res_unit[j, rows, :] = tail[:, j * UNIT : (j + 1) * UNIT]

    def unit_wait(d, j, g):
        rows = group_rows(g, 1 if g == 0 else 0)
        return remote(
            res_unit.at[j, rows], back_unit.at[d, j, rows],
            unit_send.at[j, g], unit_recv.at[d, j, g], sibling,
        )

    def unit_keep(j):
        return pltpu.make_async_copy(
            res_unit.at[j, rows_of(0)], back_unit.at[0, j, rows_of(mine)], unit_self.at[j]
        )

    def unit_hand(j):
        return remote(
            res_unit.at[j, rows_of(0)], back_unit.at[1, j, rows_of(mine)],
            unit_near.at[j], unit_far.at[j], following,
        )

    def unit_columns(j):
        return pl.ds(pl.multiple_of(begin + j * UNIT, UNIT), UNIT)

    def unit_onward(j):
        return remote(
            out_unit.at[j], out_ref.at[:, unit_columns(j)],
            unit_out_send.at[j], unit_out_recv.at[j], following,
        )

    def unit_store(j):
        return pltpu.make_async_copy(out_unit.at[UNITS + j], out_ref.at[:, unit_columns(j)], far_out.at[j])

    def unit_home(j, carry):
        d = (j >= passed).astype(jnp.int32)
        where = lax.rem(section + d, sections)
        for g, (low, high) in enumerate(GROUPS):

            def home(i, inner, g=g):
                py, px = peer(i, -1)
                remote(
                    res_unit.at[j, rows_of(i)], back_unit.at[d, j, rows_of(mine)],
                    unit_send.at[j, g], unit_recv.at[d, j, g], device(py, px, where),
                ).start()
                return inner

            lax.fori_loop(max(low, 1), high, home, 0)

        @pl.when(j < passed)
        def _():
            unit_keep(j).start()

        @pl.when(j >= passed)
        def _():
            unit_hand(j).start()

        return carry

    with jax.named_scope("p_unithome"):
        lax.fori_loop(0, UNITS, unit_home, 0)

    onward = [
        remote(
            outb[c], out_ref.at[:, pl.ds(STARTS[c], WIDTHS[c])], out_send.at[c], out_recv.at[c], following
        )
        for c in range(chunks)
    ]
    for c in range(chunks):
        with jax.named_scope("p_came"):
            keep(c).wait()
            for g in range(len(GROUPS)):
                home_copy(c, g).wait_recv()
        with jax.named_scope("p_mix"):
            part = pl.ds(STARTS[c], WIDTHS[c])
            total = x_ref[:, part].astype(jnp.float32) + mixed(mix, back[c][...])
            outb[c][...] = total.astype(jnp.bfloat16)
            onward[c].start()

    def unit_finish(j, carry):
        unit_keep(j).wait()
        for g in range(len(GROUPS)):
            unit_wait(0, j, g).wait_recv()
        total = x_ref[:, unit_columns(j)].astype(jnp.float32) + mixed(mix, back_unit[0, j])
        out_unit[j] = total.astype(jnp.bfloat16)
        unit_onward(j).start()
        return carry

    def unit_finish_far(j, carry):
        unit_hand(j).wait_recv()
        for g in range(len(GROUPS)):
            unit_wait(1, j, g).wait_recv()
        part = pl.ds(pl.multiple_of(j * UNIT, UNIT), UNIT)
        total = x_far[:, part].astype(jnp.float32) + mixed(mix_far, back_unit[1, j])
        out_unit[UNITS + j] = total.astype(jnp.bfloat16)
        unit_store(j).start()
        return carry

    with jax.named_scope("p_unitfin"):
        lax.fori_loop(0, passed, unit_finish, 0)
    @pl.when(taken < UNITS)
    def _():
        for copy in far_copies:
            copy.wait_recv()
        fill_mix(mix_far, *places(routes_far[...]), gates_far[...])

    with jax.named_scope("p_unitfar"):
        lax.fori_loop(taken, UNITS, unit_finish_far, 0)

    for j in range(2):
        beside_copies[j].wait_send()
        forward_copies[j].wait_send()
    with jax.named_scope("p_drain"):
        for g in range(len(GROUPS)):
            went(g).wait_send()
            for c in range(chunks):
                home_copy(c, g).wait_send()
        for c in range(chunks):
            onward[c].wait()

        def drain_sent(j, carry):
            for g in range(len(GROUPS)):
                unit_wait(0, j, g).wait_send()
            return carry

        def drain_onward(j, carry):
            unit_onward(j).wait_send()
            return carry

        def drain_hand(j, carry):
            unit_hand(j).wait_send()
            return carry

        def drain_came(j, carry):
            unit_onward(j).wait_recv()
            return carry

        def drain_store(j, carry):
            unit_store(j).wait()
            return carry

        lax.fori_loop(0, UNITS, drain_sent, 0)
        lax.fori_loop(0, passed, drain_onward, 0)
        lax.fori_loop(passed, UNITS, drain_hand, 0)
        lax.fori_loop(0, taken, drain_came, 0)
        lax.fori_loop(taken, UNITS, drain_store, 0)

        @pl.when(passed < UNITS)
        def _():
            for copy in far_copies:
                copy.wait_send()


def shards(carried, norm_gain, w_up, w_down, routes, gate_weights):
    tokens, width = carried.shape[1:]
    quarter = w_down.shape[1]
    slots = EXPERTS * 32
    bf16 = jnp.bfloat16
    dma = pltpu.SemaphoreType.DMA
    whole = pl.BlockSpec(memory_space=pl.ANY)
    chunks = len(WIDTHS)
    out = pl.pallas_call(
        kernel,
        name="section_layer",
        out_shape=jax.ShapeDtypeStruct((tokens, width), bf16),
        in_specs=[whole] * 6,
        out_specs=whole,
        scratch_shapes=[
            pltpu.VMEM((tokens, width), bf16),
            pltpu.VMEM((1, width), jnp.float32),
            pltpu.VMEM((2, tokens), jnp.int32),
            pltpu.VMEM((2, tokens), jnp.float32),
            pltpu.VMEM((4 * quarter, width), bf16),
            pltpu.VMEM((4 * quarter, width), bf16),
            pltpu.VMEM((tokens, width), bf16),
            pltpu.VMEM((slots, width), bf16),
            pltpu.VMEM((slots, width), bf16),
            pltpu.VMEM((slots, 4 * quarter), bf16),
            pltpu.VMEM((tokens, 2 * slots), bf16),
            pltpu.VMEM((tokens, UNITS * UNIT), bf16),
            pltpu.VMEM((2, tokens), jnp.int32),
            pltpu.VMEM((2, tokens), jnp.float32),
            pltpu.VMEM((tokens, 2 * slots), bf16),
            pltpu.VMEM((UNITS, slots, UNIT), bf16),
            pltpu.VMEM((2, UNITS, slots, UNIT), bf16),
            pltpu.VMEM((2 * UNITS, tokens, UNIT), bf16),
            *[pltpu.VMEM((slots, w), bf16) for w in WIDTHS],
            *[pltpu.VMEM((slots, w), bf16) for w in WIDTHS],
            *[pltpu.VMEM((tokens, w), bf16) for w in WIDTHS],
            dma((4,)), dma((2,)), dma((2,)), dma((2,)), dma((2,)), dma((2,)), dma((2,)), dma((2,)),
            dma, dma((len(GROUPS),)), dma((len(GROUPS),)),
            dma((chunks,)), dma((chunks, len(GROUPS))), dma((chunks, len(GROUPS))),
            dma((chunks,)), dma((chunks,)),
            dma((3,)), dma((3,)), dma((UNITS,)), dma((UNITS, len(GROUPS))), dma((2, UNITS, len(GROUPS))),
            dma((UNITS,)), dma((UNITS,)), dma((UNITS,)), dma((UNITS,)), dma((UNITS,)),
            pltpu.SemaphoreType.REGULAR, pltpu.SemaphoreType.REGULAR,
        ],
        compiler_params=pltpu.CompilerParams(
            collective_id=0, has_side_effects=True, vmem_limit_bytes=56 * 1024 * 1024
        ),
        cost_estimate=pl.CostEstimate(
            flops=16 * slots * width * quarter, bytes_accessed=8 * quarter * width, transcendentals=0
        ),
    )(carried[0], norm_gain, w_up[0].T, w_down[0], routes[0, 0].T, gate_weights[0, 0].T)
    return out[None]


def solution(mesh):
    in_specs = (
        P("section", "expert", None),
        P("section", None),
        P("section", None, "expert"),
        P("section", "expert", None),
        P(None, "section", "expert", None),
        P(None, "section", "expert", None),
    )
    return jax.shard_map(
        shards, mesh=mesh, in_specs=in_specs, out_specs=P("section", "expert", None), check_vma=False
    )
```

```python
import jax
import jax.numpy as jnp
from jax import lax
from jax.experimental import pallas as pl
from jax.experimental.pallas import tpu as pltpu
from jax.sharding import PartitionSpec as P

MESH = pl.DeviceIdType.MESH
NX, NY, NC = 4, 8, 2
PEERS = 2 * NY
EXPERTS = NX * NY // 2
GROUPS = ((0, 10), (10, 16))
WIDTHS = (512, 512, 256, 128)
UNITS, UNIT = 5, 128
DIRECT = 6
STARTS = tuple(sum(WIDTHS[:c]) for c in range(len(WIDTHS)))


def kernel(
    x_hbm, gain_hbm, up_ref, down_ref, routes_hbm, gates_hbm, out_ref,
    x_ref, gain_ref, routes_ref, gates_ref,
    up_all, down_all, normed, send, recv, hidden, mix,
    x_far, routes_far, gates_far, mix_far, res_unit, back_unit, out_unit, relay, *rest,
):
    chunks = len(WIDTHS)
    res, back, outb = rest[:chunks], rest[chunks : 2 * chunks], rest[2 * chunks : 3 * chunks]
    (
        in_sem, own_sem, sib_send, sib_recv, xp_send, xp_recv, fwd_send, fwd_recv,
        self_sem, go_send, go_recv, home_self, home_send, home_recv, out_send, out_recv,
        far_send, far_recv, unit_self, unit_send, unit_recv, unit_near, unit_far, unit_out_send, unit_out_recv, far_out, ready, late_ready, relay_send, relay_recv,
    ) = rest[3 * chunks :]
    tokens, width = x_ref.shape
    quarter = up_ref.shape[0]
    slots = send.shape[0]
    cap = slots // EXPERTS
    sections = lax.axis_size("section")
    section = lax.axis_index("section")
    me = lax.axis_index("expert")
    core = lax.rem(me, NC)
    chip = lax.div(me, NC)
    x = lax.rem(chip, NX)
    y = lax.div(chip, NX)
    mine = y * 2 + lax.div(x, 2)

    def peer(i, sign):
        k = lax.div(i, 2)
        half = lax.div(k + 1, 2)
        dy = half * (2 * lax.rem(k, 2) - 1)
        return lax.rem(y + NY + sign * dy, NY), lax.rem(i, 2) * (NX - 1 - 2 * x) + x

    def device(py, px, where=section):
        return (where, (py * NX + px) * NC + core)

    sibling = (section, chip * NC + 1 - core)
    beside = (section, (chip + 1 - 2 * lax.rem(x, 2)) * NC + core)
    following = (lax.rem(section + 1, sections), me)
    previous = (lax.rem(section + sections - 1, sections), me)
    begin = STARTS[-1] + WIDTHS[-1]
    passed = UNITS - lax.min(UNITS, lax.max(0, DIRECT - lax.rem(section + 1, sections)))
    taken = UNITS - lax.min(UNITS, lax.max(0, DIRECT - section))

    last = sections - 1
    kin = (core == 0) & ((x == 0) | (x == NX - 1))
    is_late = (section == 0) & (me == 0)
    sibling_late = (section == 0) & (me == 1)
    beside_late = (section == 0) & (me == NC)
    near_late = (section == 0) & (me != 0) & (kin | (me == 1) | (me == NC))
    next_late = (section == 1) & jnp.where(taken < UNITS, kin, me == 0)
    punctual = jnp.logical_not(is_late)
    onward_count = jnp.where(passed < UNITS, PEERS, 1)
    before_count = jnp.where(taken < UNITS, PEERS, 1)

    def hello(target):
        pl.semaphore_signal(barrier, inc=1, device_id=target, device_id_type=MESH)

    barrier = pltpu.get_barrier_semaphore()
    inputs = [
        pltpu.make_async_copy(src, dst, in_sem.at[j])
        for j, (src, dst) in enumerate(
            ((routes_hbm, routes_ref), (gain_hbm, gain_ref), (x_hbm, x_ref), (gates_hbm, gates_ref))
        )
    ]
    for copy in inputs:
        copy.start()

    def greet(i, carry):
        hello(device(*peer(PEERS - i, -1)))
        return carry

    def greet_at(where, number):
        def greet_far(i, carry):
            hello(device(*peer(i, -1), where))
            return carry

        lax.fori_loop(0, number, greet_far, 0)

    @pl.when(punctual)
    def _():
        lax.fori_loop(1, PEERS, greet, 0)
        hello(sibling)
        hello(beside)

    @pl.when(punctual & (section < last))
    def _():
        greet_at(section + 1, onward_count)

    @pl.when(section == 0)
    def _():
        greet_at(last, before_count)

    @pl.when(next_late)
    def _():
        hello((0, 0))

    @pl.when(sibling_late)
    def _():
        def greet_for(i, carry):
            py, px = peer(i, -1)
            hello((section, (py * NX + px) * NC))
            return carry

        lax.fori_loop(1, PEERS, greet_for, 0)

    own = [
        pltpu.make_async_copy(src, dst.at[pl.ds(0, quarter)], own_sem.at[j])
        for j, (src, dst) in enumerate(((up_ref, up_all), (down_ref, down_all)))
    ]
    for copy in own:
        copy.start()

    def places(ids):
        names = lax.broadcasted_iota(jnp.int32, (EXPERTS, tokens), 0)
        first = (names == ids[0:1, :]).astype(jnp.float32)
        second = (names == ids[1:2, :]).astype(jnp.float32)
        earlier = (
            lax.broadcasted_iota(jnp.int32, (tokens, tokens), 0)
            < lax.broadcasted_iota(jnp.int32, (tokens, tokens), 1)
        ).astype(jnp.bfloat16)
        count = jnp.dot(
            (first + second).astype(jnp.bfloat16), earlier, preferred_element_type=jnp.float32
        )
        place0 = jnp.sum(count * first, axis=0, keepdims=True).astype(jnp.int32) + ids[0:1, :] * cap
        place1 = jnp.sum(count * second, axis=0, keepdims=True).astype(jnp.int32) + ids[1:2, :] * cap
        slot = lax.broadcasted_iota(jnp.int32, (slots, tokens), 0)
        return slot == place0, slot == place1

    def fill_mix(mix, is0, is1, gates):
        weight = jnp.where(is0, gates[0:1, :], 0.0) + jnp.where(is1, gates[1:2, :], 0.0)
        weight = weight.T
        high_part = weight.astype(jnp.bfloat16)
        mix[:, pl.ds(0, slots)] = high_part
        mix[:, pl.ds(slots, slots)] = (weight - high_part.astype(jnp.float32)).astype(jnp.bfloat16)

    def mixed(mix, rows):
        total = jnp.dot(mix[:, pl.ds(0, slots)], rows, preferred_element_type=jnp.float32)
        return total + jnp.dot(mix[:, pl.ds(slots, slots)], rows, preferred_element_type=jnp.float32)

    inputs[0].wait()
    is0, is1 = places(routes_ref[...])
    assign = (is0 | is1).astype(jnp.float32).astype(jnp.bfloat16)

    block = 48

    def norm(i, carry):
        rows = pl.ds(pl.multiple_of(i * block, 16), block)
        values = x_ref[rows, :].astype(jnp.float32)
        inverse = lax.rsqrt(jnp.mean(values * values, axis=-1, keepdims=True) + 1e-05)
        normed[rows, :] = (values * inverse * gain_ref[...]).astype(jnp.bfloat16)
        return carry

    inputs[1].wait()
    inputs[2].wait()
    with jax.named_scope("p_norm"):
        lax.fori_loop(0, tokens // block, norm, 0)

    piece = 512

    def fill(i, carry):
        part = pl.ds(pl.multiple_of(i * piece, piece), piece)
        send[:, part] = jnp.dot(
            assign, normed[:, part], preferred_element_type=jnp.float32
        ).astype(jnp.bfloat16)
        return carry

    with jax.named_scope("p_fill"):
        lax.fori_loop(0, width // piece, fill, 0)

    with jax.named_scope("p_barrier"):
        pl.semaphore_wait(
            barrier,
            PEERS + 1
            - (sibling_late | beside_late).astype(jnp.int32)
            + jnp.where(section > 0, before_count, 0)
            - next_late.astype(jnp.int32)
            + jnp.where((section == last) | is_late, onward_count, 0),
        )

    def remote(src, dst, send_sem, recv_sem, target):
        return pltpu.make_async_remote_copy(
            src_ref=src, dst_ref=dst, send_sem=send_sem, recv_sem=recv_sem,
            device_id=target, device_id_type=MESH,
        )

    def rows_of(which):
        return pl.ds(pl.multiple_of(which * cap, cap), cap)

    def group_rows(g, skip=0):
        low, high = GROUPS[g]
        return pl.ds((low + skip) * cap, (high - low - skip) * cap)

    weights = ((up_ref, up_all), (down_ref, down_all))
    beside_copies = [
        remote(src, dst.at[pl.ds(2 * quarter, quarter)], xp_send.at[j], xp_recv.at[j], beside)
        for j, (src, dst) in enumerate(weights)
    ]
    sibling_copies = [
        remote(src, dst.at[pl.ds(quarter, quarter)], sib_send.at[j], sib_recv.at[j], sibling)
        for j, (src, dst) in enumerate(weights)
    ]
    @pl.when(is_late)
    def _():
        def arrived(target):
            pl.semaphore_signal(late_ready, inc=1, device_id=target, device_id_type=MESH)

        def tell_peer(i, carry):
            arrived(device(*peer(i, 1)))
            return carry

        lax.fori_loop(1, PEERS, tell_peer, 0)
        arrived(sibling)
        arrived(beside)

    def launch(copies, here):
        @pl.when(here)
        def _():
            for copy in copies:
                copy.start()

    launch(beside_copies, jnp.logical_not(beside_late))
    for g, (low, high) in enumerate(GROUPS):

        def go(i, carry, g=g):
            py, px = peer(i, 1)
            target = device(py, px)
            source = send.at[rows_of(py * 2 + lax.div(px, 2))]
            to_late = (section == 0) & (target[1] == 0)

            @pl.when(jnp.logical_not(to_late))
            def _():
                remote(source, recv.at[rows_of(i)], go_send.at[g], go_recv.at[g], target).start()

            @pl.when(to_late)
            def _():
                remote(source, relay.at[rows_of(i)], go_send.at[g], relay_recv.at[g], (section, 1)).start()

            return carry

        lax.fori_loop(max(low, 1), high, go, 0)

    stay = pltpu.make_async_copy(send.at[rows_of(mine)], recv.at[rows_of(0)], self_sem)
    stay.start()

    @pl.when(section > 0)
    def _():
        def tell(i, carry):
            target = device(*peer(i, 1), section - 1)

            @pl.when(jnp.logical_not((section == 1) & (target[1] == 0)))
            def _():
                pl.semaphore_signal(ready, inc=1, device_id=target, device_id_type=MESH)

            return carry

        lax.fori_loop(0, before_count, tell, 0)

    launch(sibling_copies, jnp.logical_not(sibling_late))
    inputs[3].wait()
    far_copies = [
        remote(src, dst, far_send.at[j], far_recv.at[j], following)
        for j, (src, dst) in enumerate(
            (
                (routes_ref, routes_far),
                (gates_ref, gates_far),
                (x_ref.at[:, pl.ds(begin, UNITS * UNIT)], x_far),
            )
        )
    ]

    fill_mix(mix, is0, is1, gates_ref[...])

    @pl.when(punctual & (section < last))
    def _():
        pl.semaphore_wait(ready, onward_count)

    @pl.when(passed < UNITS)
    def _():
        for copy in far_copies:
            copy.start()

    @pl.when(near_late)
    def _():
        pl.semaphore_wait(late_ready, 1)

    launch(beside_copies, beside_late)
    launch(sibling_copies, sibling_late)

    forward_copies = [
        remote(
            dst.at[pl.ds(2 * quarter, quarter)], dst.at[pl.ds(3 * quarter, quarter)],
            fwd_send.at[j], fwd_recv.at[j], sibling,
        )
        for j, (_, dst) in enumerate(weights)
    ]
    for copy in own:
        copy.wait()
    for copy in sibling_copies:
        copy.wait()
    stay.wait()

    def went(g):
        rows = group_rows(g, 1 if g == 0 else 0)
        return remote(send.at[rows], recv.at[rows], go_send.at[g], go_recv.at[g], sibling)

    def home_copy(c, g):
        rows = group_rows(g, 1 if g == 0 else 0)
        return remote(res[c].at[rows], back[c].at[rows], home_send.at[c, g], home_recv.at[c, g], sibling)

    def keep(c):
        return pltpu.make_async_copy(res[c].at[rows_of(0)], back[c].at[rows_of(mine)], home_self.at[c])

    def passing(g):
        rows = group_rows(g, 1 if g == 0 else 0)
        return remote(relay.at[rows], recv.at[rows], relay_send.at[g], go_recv.at[g], sibling)

    def came_to_pass(g):
        rows = group_rows(g, 1 if g == 0 else 0)
        return remote(send.at[rows], relay.at[rows], go_send.at[g], relay_recv.at[g], sibling)

    for j in range(2):
        with jax.named_scope(f"p_beside{j}"):
            beside_copies[j].wait_recv()
            forward_copies[j].start()
    units = 256
    for g, (low, high) in enumerate(GROUPS):
        rows = group_rows(g)
        with jax.named_scope("p_arrive"):
            went(g).wait_recv()

        @pl.when(sibling_late)
        def _(g=g):
            came_to_pass(g).wait_recv()
            passing(g).start()

        if g == 0:
            with jax.named_scope("p_fwd0"):
                forward_copies[0].wait_recv()

        def up(i, carry, rows=rows):
            part = pl.ds(pl.multiple_of(i * units, units), units)
            v = lax.dot_general(
                recv[rows, :], up_all[part, :], (((1,), (1,)), ((), ())),
                preferred_element_type=jnp.float32,
            )
            inner = 0.7978845608028654 * (v + 0.044715 * (v * v * v))
            hidden[rows, part] = (0.5 * v * (1.0 + jnp.tanh(inner))).astype(jnp.bfloat16)
            return carry

        with jax.named_scope("p_up"):
            lax.fori_loop(0, 4 * quarter // units, up, 0)
        if g == 0:
            with jax.named_scope("p_fwd1"):
                forward_copies[1].wait_recv()
        for c in range(chunks):
            with jax.named_scope("p_down"):
                res[c][rows, :] = jnp.dot(
                    hidden[rows, :], down_all[:, pl.ds(STARTS[c], WIDTHS[c])],
                    preferred_element_type=jnp.float32,
                ).astype(jnp.bfloat16)

            def home(i, carry, c=c, g=g):
                py, px = peer(i, -1)
                remote(
                    res[c].at[rows_of(i)], back[c].at[rows_of(mine)],
                    home_send.at[c, g], home_recv.at[c, g], device(py, px),
                ).start()
                return carry

            with jax.named_scope("p_home"):
                lax.fori_loop(max(low, 1), high, home, 0)
            if g == 0:
                keep(c).start()
        tail = jnp.dot(
            hidden[rows, :], down_all[:, pl.ds(begin, UNITS * UNIT)], preferred_element_type=jnp.float32
        ).astype(jnp.bfloat16)
        for j in range(UNITS):
            res_unit[j, rows, :] = tail[:, j * UNIT : (j + 1) * UNIT]

    def unit_wait(d, j, g):
        rows = group_rows(g, 1 if g == 0 else 0)
        return remote(
            res_unit.at[j, rows], back_unit.at[d, j, rows],
            unit_send.at[j, g], unit_recv.at[d, j, g], sibling,
        )

    def unit_keep(j):
        return pltpu.make_async_copy(
            res_unit.at[j, rows_of(0)], back_unit.at[0, j, rows_of(mine)], unit_self.at[j]
        )

    def unit_hand(j):
        return remote(
            res_unit.at[j, rows_of(0)], back_unit.at[1, j, rows_of(mine)],
            unit_near.at[j], unit_far.at[j], following,
        )

    def unit_columns(j):
        return pl.ds(pl.multiple_of(begin + j * UNIT, UNIT), UNIT)

    def unit_onward(j):
        return remote(
            out_unit.at[j], out_ref.at[:, unit_columns(j)],
            unit_out_send.at[j], unit_out_recv.at[j], following,
        )

    def unit_store(j):
        return pltpu.make_async_copy(out_unit.at[UNITS + j], out_ref.at[:, unit_columns(j)], far_out.at[j])

    def unit_home(j, carry):
        d = (j >= passed).astype(jnp.int32)
        where = lax.rem(section + d, sections)
        for g, (low, high) in enumerate(GROUPS):

            def home(i, inner, g=g):
                py, px = peer(i, -1)
                remote(
                    res_unit.at[j, rows_of(i)], back_unit.at[d, j, rows_of(mine)],
                    unit_send.at[j, g], unit_recv.at[d, j, g], device(py, px, where),
                ).start()
                return inner

            lax.fori_loop(max(low, 1), high, home, 0)

        @pl.when(j < passed)
        def _():
            unit_keep(j).start()

        @pl.when(j >= passed)
        def _():
            unit_hand(j).start()

        return carry

    with jax.named_scope("p_unithome"):
        lax.fori_loop(0, UNITS, unit_home, 0)

    onward = [
        remote(
            outb[c], out_ref.at[:, pl.ds(STARTS[c], WIDTHS[c])], out_send.at[c], out_recv.at[c], following
        )
        for c in range(chunks)
    ]
    for c in range(chunks):
        with jax.named_scope("p_came"):
            keep(c).wait()
            for g in range(len(GROUPS)):
                home_copy(c, g).wait_recv()
        with jax.named_scope("p_mix"):
            part = pl.ds(STARTS[c], WIDTHS[c])
            total = x_ref[:, part].astype(jnp.float32) + mixed(mix, back[c][...])
            outb[c][...] = total.astype(jnp.bfloat16)
            onward[c].start()

    def unit_finish(j, carry):
        unit_keep(j).wait()
        for g in range(len(GROUPS)):
            unit_wait(0, j, g).wait_recv()
        total = x_ref[:, unit_columns(j)].astype(jnp.float32) + mixed(mix, back_unit[0, j])
        out_unit[j] = total.astype(jnp.bfloat16)
        unit_onward(j).start()
        return carry

    def unit_finish_far(j, carry):
        unit_hand(j).wait_recv()
        for g in range(len(GROUPS)):
            unit_wait(1, j, g).wait_recv()
        part = pl.ds(pl.multiple_of(j * UNIT, UNIT), UNIT)
        total = x_far[:, part].astype(jnp.float32) + mixed(mix_far, back_unit[1, j])
        out_unit[UNITS + j] = total.astype(jnp.bfloat16)
        unit_store(j).start()
        return carry

    with jax.named_scope("p_unitfin"):
        lax.fori_loop(0, passed, unit_finish, 0)
    @pl.when(taken < UNITS)
    def _():
        for copy in far_copies:
            copy.wait_recv()
        fill_mix(mix_far, *places(routes_far[...]), gates_far[...])

    with jax.named_scope("p_unitfar"):
        lax.fori_loop(taken, UNITS, unit_finish_far, 0)

    for j in range(2):
        beside_copies[j].wait_send()
        forward_copies[j].wait_send()
    with jax.named_scope("p_drain"):
        for g in range(len(GROUPS)):
            went(g).wait_send()

            @pl.when(sibling_late)
            def _(g=g):
                passing(g).wait_send()

            for c in range(chunks):
                home_copy(c, g).wait_send()
        for c in range(chunks):
            onward[c].wait()

        def drain_sent(j, carry):
            for g in range(len(GROUPS)):
                unit_wait(0, j, g).wait_send()
            return carry

        def drain_onward(j, carry):
            unit_onward(j).wait_send()
            return carry

        def drain_hand(j, carry):
            unit_hand(j).wait_send()
            return carry

        def drain_came(j, carry):
            unit_onward(j).wait_recv()
            return carry

        def drain_store(j, carry):
            unit_store(j).wait()
            return carry

        lax.fori_loop(0, UNITS, drain_sent, 0)
        lax.fori_loop(0, passed, drain_onward, 0)
        lax.fori_loop(passed, UNITS, drain_hand, 0)
        lax.fori_loop(0, taken, drain_came, 0)
        lax.fori_loop(taken, UNITS, drain_store, 0)

        @pl.when(passed < UNITS)
        def _():
            for copy in far_copies:
                copy.wait_send()


def shards(carried, norm_gain, w_up, w_down, routes, gate_weights):
    tokens, width = carried.shape[1:]
    quarter = w_down.shape[1]
    slots = EXPERTS * 32
    bf16 = jnp.bfloat16
    dma = pltpu.SemaphoreType.DMA
    whole = pl.BlockSpec(memory_space=pl.ANY)
    chunks = len(WIDTHS)
    out = pl.pallas_call(
        kernel,
        name="section_layer",
        out_shape=jax.ShapeDtypeStruct((tokens, width), bf16),
        in_specs=[whole] * 6,
        out_specs=whole,
        scratch_shapes=[
            pltpu.VMEM((tokens, width), bf16),
            pltpu.VMEM((1, width), jnp.float32),
            pltpu.VMEM((2, tokens), jnp.int32),
            pltpu.VMEM((2, tokens), jnp.float32),
            pltpu.VMEM((4 * quarter, width), bf16),
            pltpu.VMEM((4 * quarter, width), bf16),
            pltpu.VMEM((tokens, width), bf16),
            pltpu.VMEM((slots, width), bf16),
            pltpu.VMEM((slots, width), bf16),
            pltpu.VMEM((slots, 4 * quarter), bf16),
            pltpu.VMEM((tokens, 2 * slots), bf16),
            pltpu.VMEM((tokens, UNITS * UNIT), bf16),
            pltpu.VMEM((2, tokens), jnp.int32),
            pltpu.VMEM((2, tokens), jnp.float32),
            pltpu.VMEM((tokens, 2 * slots), bf16),
            pltpu.VMEM((UNITS, slots, UNIT), bf16),
            pltpu.VMEM((2, UNITS, slots, UNIT), bf16),
            pltpu.VMEM((2 * UNITS, tokens, UNIT), bf16),
            pltpu.VMEM((slots, width), bf16),
            *[pltpu.VMEM((slots, w), bf16) for w in WIDTHS],
            *[pltpu.VMEM((slots, w), bf16) for w in WIDTHS],
            *[pltpu.VMEM((tokens, w), bf16) for w in WIDTHS],
            dma((4,)), dma((2,)), dma((2,)), dma((2,)), dma((2,)), dma((2,)), dma((2,)), dma((2,)),
            dma, dma((len(GROUPS),)), dma((len(GROUPS),)),
            dma((chunks,)), dma((chunks, len(GROUPS))), dma((chunks, len(GROUPS))),
            dma((chunks,)), dma((chunks,)),
            dma((3,)), dma((3,)), dma((UNITS,)), dma((UNITS, len(GROUPS))), dma((2, UNITS, len(GROUPS))),
            dma((UNITS,)), dma((UNITS,)), dma((UNITS,)), dma((UNITS,)), dma((UNITS,)),
            pltpu.SemaphoreType.REGULAR, pltpu.SemaphoreType.REGULAR, dma((len(GROUPS),)), dma((len(GROUPS),)),
        ],
        compiler_params=pltpu.CompilerParams(
            collective_id=0, has_side_effects=True, vmem_limit_bytes=56 * 1024 * 1024
        ),
        cost_estimate=pl.CostEstimate(
            flops=16 * slots * width * quarter, bytes_accessed=8 * quarter * width, transcendentals=0
        ),
    )(carried[0], norm_gain, w_up[0].T, w_down[0], routes[0, 0].T, gate_weights[0, 0].T)
    return out[None]


def solution(mesh):
    in_specs = (
        P("section", "expert", None),
        P("section", None),
        P("section", None, "expert"),
        P("section", "expert", None),
        P(None, "section", "expert", None),
        P(None, "section", "expert", None),
    )
    return jax.shard_map(
        shards, mesh=mesh, in_specs=in_specs, out_specs=P("section", "expert", None), check_vma=False
    )
```

```python
import jax
import jax.numpy as jnp
from jax import lax
from jax.experimental import pallas as pl
from jax.experimental.pallas import tpu as pltpu
from jax.sharding import PartitionSpec as P

MESH = pl.DeviceIdType.MESH
NX, NY, NC = 4, 8, 2
PEERS = 2 * NY
EXPERTS = NX * NY // 2
GROUPS = ((0, 10), (10, 16))
WIDTHS = (384, 384, 256, 256, 128)
UNITS, UNIT = 5, 128
DIRECT = 6
STARTS = tuple(sum(WIDTHS[:c]) for c in range(len(WIDTHS)))


def kernel(
    x_hbm, gain_hbm, up_ref, down_ref, routes_hbm, gates_hbm, out_ref,
    x_ref, gain_ref, routes_ref, gates_ref,
    up_all, down_all, normed, send, recv, hidden, mix,
    x_far, routes_far, gates_far, mix_far, res_unit, back_unit, out_unit, relay, *rest,
):
    chunks = len(WIDTHS)
    res, back, outb = rest[:chunks], rest[chunks : 2 * chunks], rest[2 * chunks : 3 * chunks]
    (
        in_sem, own_sem, sib_send, sib_recv, xp_send, xp_recv, fwd_send, fwd_recv,
        self_sem, go_send, go_recv, home_self, home_send, home_recv, out_send, out_recv,
        far_send, far_recv, unit_self, unit_send, unit_recv, unit_near, unit_far, unit_out_send, unit_out_recv, far_out, ready, late_ready, relay_send, relay_recv,
    ) = rest[3 * chunks :]
    tokens, width = x_ref.shape
    quarter = up_ref.shape[0]
    slots = send.shape[0]
    cap = slots // EXPERTS
    sections = lax.axis_size("section")
    section = lax.axis_index("section")
    me = lax.axis_index("expert")
    core = lax.rem(me, NC)
    chip = lax.div(me, NC)
    x = lax.rem(chip, NX)
    y = lax.div(chip, NX)
    mine = y * 2 + lax.div(x, 2)

    def peer(i, sign):
        k = lax.div(i, 2)
        half = lax.div(k + 1, 2)
        dy = half * (2 * lax.rem(k, 2) - 1)
        return lax.rem(y + NY + sign * dy, NY), lax.rem(i, 2) * (NX - 1 - 2 * x) + x

    def device(py, px, where=section):
        return (where, (py * NX + px) * NC + core)

    sibling = (section, chip * NC + 1 - core)
    beside = (section, (chip + 1 - 2 * lax.rem(x, 2)) * NC + core)
    following = (lax.rem(section + 1, sections), me)
    previous = (lax.rem(section + sections - 1, sections), me)
    begin = STARTS[-1] + WIDTHS[-1]
    passed = UNITS - lax.min(UNITS, lax.max(0, DIRECT - lax.rem(section + 1, sections)))
    taken = UNITS - lax.min(UNITS, lax.max(0, DIRECT - section))

    last = sections - 1
    kin = (core == 0) & ((x == 0) | (x == NX - 1))
    is_late = (section == 0) & (me == 0)
    sibling_late = (section == 0) & (me == 1)
    beside_late = (section == 0) & (me == NC)
    near_late = (section == 0) & (me != 0) & (kin | (me == 1) | (me == NC))
    next_late = (section == 1) & jnp.where(taken < UNITS, kin, me == 0)
    punctual = jnp.logical_not(is_late)
    onward_count = jnp.where(passed < UNITS, PEERS, 1)
    before_count = jnp.where(taken < UNITS, PEERS, 1)

    def hello(target):
        pl.semaphore_signal(barrier, inc=1, device_id=target, device_id_type=MESH)

    barrier = pltpu.get_barrier_semaphore()
    inputs = [
        pltpu.make_async_copy(src, dst, in_sem.at[j])
        for j, (src, dst) in enumerate(
            ((routes_hbm, routes_ref), (gain_hbm, gain_ref), (x_hbm, x_ref), (gates_hbm, gates_ref))
        )
    ]
    for copy in inputs:
        copy.start()

    def greet(i, carry):
        hello(device(*peer(PEERS - i, -1)))
        return carry

    def greet_at(where, number):
        def greet_far(i, carry):
            hello(device(*peer(i, -1), where))
            return carry

        lax.fori_loop(0, number, greet_far, 0)

    @pl.when(punctual)
    def _():
        lax.fori_loop(1, PEERS, greet, 0)
        hello(sibling)
        hello(beside)

    @pl.when(punctual & (section < last))
    def _():
        greet_at(section + 1, onward_count)

    @pl.when(section == 0)
    def _():
        greet_at(last, before_count)

    @pl.when(next_late)
    def _():
        hello((0, 0))

    @pl.when(sibling_late)
    def _():
        def greet_for(i, carry):
            py, px = peer(i, -1)
            hello((section, (py * NX + px) * NC))
            return carry

        lax.fori_loop(1, PEERS, greet_for, 0)

    own = [
        pltpu.make_async_copy(src, dst.at[pl.ds(0, quarter)], own_sem.at[j])
        for j, (src, dst) in enumerate(((up_ref, up_all), (down_ref, down_all)))
    ]
    for copy in own:
        copy.start()

    def places(ids):
        names = lax.broadcasted_iota(jnp.int32, (EXPERTS, tokens), 0)
        first = (names == ids[0:1, :]).astype(jnp.float32)
        second = (names == ids[1:2, :]).astype(jnp.float32)
        earlier = (
            lax.broadcasted_iota(jnp.int32, (tokens, tokens), 0)
            < lax.broadcasted_iota(jnp.int32, (tokens, tokens), 1)
        ).astype(jnp.bfloat16)
        count = jnp.dot(
            (first + second).astype(jnp.bfloat16), earlier, preferred_element_type=jnp.float32
        )
        place0 = jnp.sum(count * first, axis=0, keepdims=True).astype(jnp.int32) + ids[0:1, :] * cap
        place1 = jnp.sum(count * second, axis=0, keepdims=True).astype(jnp.int32) + ids[1:2, :] * cap
        slot = lax.broadcasted_iota(jnp.int32, (slots, tokens), 0)
        return slot == place0, slot == place1

    def fill_mix(mix, is0, is1, gates):
        weight = jnp.where(is0, gates[0:1, :], 0.0) + jnp.where(is1, gates[1:2, :], 0.0)
        weight = weight.T
        high_part = weight.astype(jnp.bfloat16)
        mix[:, pl.ds(0, slots)] = high_part
        mix[:, pl.ds(slots, slots)] = (weight - high_part.astype(jnp.float32)).astype(jnp.bfloat16)

    def mixed(mix, rows):
        total = jnp.dot(mix[:, pl.ds(0, slots)], rows, preferred_element_type=jnp.float32)
        return total + jnp.dot(mix[:, pl.ds(slots, slots)], rows, preferred_element_type=jnp.float32)

    inputs[0].wait()
    is0, is1 = places(routes_ref[...])
    assign = (is0 | is1).astype(jnp.float32).astype(jnp.bfloat16)

    block = 48

    def norm(i, carry):
        rows = pl.ds(pl.multiple_of(i * block, 16), block)
        values = x_ref[rows, :].astype(jnp.float32)
        inverse = lax.rsqrt(jnp.mean(values * values, axis=-1, keepdims=True) + 1e-05)
        normed[rows, :] = (values * inverse * gain_ref[...]).astype(jnp.bfloat16)
        return carry

    inputs[1].wait()
    inputs[2].wait()
    with jax.named_scope("p_norm"):
        lax.fori_loop(0, tokens // block, norm, 0)

    piece = 512

    def fill(i, carry):
        part = pl.ds(pl.multiple_of(i * piece, piece), piece)
        send[:, part] = jnp.dot(
            assign, normed[:, part], preferred_element_type=jnp.float32
        ).astype(jnp.bfloat16)
        return carry

    with jax.named_scope("p_fill"):
        lax.fori_loop(0, width // piece, fill, 0)

    with jax.named_scope("p_barrier"):
        pl.semaphore_wait(
            barrier,
            PEERS + 1
            - (sibling_late | beside_late).astype(jnp.int32)
            + jnp.where(section > 0, before_count, 0)
            - next_late.astype(jnp.int32)
            + jnp.where((section == last) | is_late, onward_count, 0),
        )

    def remote(src, dst, send_sem, recv_sem, target):
        return pltpu.make_async_remote_copy(
            src_ref=src, dst_ref=dst, send_sem=send_sem, recv_sem=recv_sem,
            device_id=target, device_id_type=MESH,
        )

    def rows_of(which):
        return pl.ds(pl.multiple_of(which * cap, cap), cap)

    def group_rows(g, skip=0):
        low, high = GROUPS[g]
        return pl.ds((low + skip) * cap, (high - low - skip) * cap)

    weights = ((up_ref, up_all), (down_ref, down_all))
    beside_copies = [
        remote(src, dst.at[pl.ds(2 * quarter, quarter)], xp_send.at[j], xp_recv.at[j], beside)
        for j, (src, dst) in enumerate(weights)
    ]
    sibling_copies = [
        remote(src, dst.at[pl.ds(quarter, quarter)], sib_send.at[j], sib_recv.at[j], sibling)
        for j, (src, dst) in enumerate(weights)
    ]
    @pl.when(is_late)
    def _():
        def arrived(target):
            pl.semaphore_signal(late_ready, inc=1, device_id=target, device_id_type=MESH)

        def tell_peer(i, carry):
            arrived(device(*peer(i, 1)))
            return carry

        lax.fori_loop(1, PEERS, tell_peer, 0)
        arrived(sibling)
        arrived(beside)

    def launch(copies, here):
        @pl.when(here)
        def _():
            for copy in copies:
                copy.start()

    launch(beside_copies, jnp.logical_not(beside_late))
    for g, (low, high) in enumerate(GROUPS):

        def go(i, carry, g=g):
            py, px = peer(i, 1)
            target = device(py, px)
            source = send.at[rows_of(py * 2 + lax.div(px, 2))]
            to_late = (section == 0) & (target[1] == 0)

            @pl.when(jnp.logical_not(to_late))
            def _():
                remote(source, recv.at[rows_of(i)], go_send.at[g], go_recv.at[g], target).start()

            @pl.when(to_late)
            def _():
                remote(source, relay.at[rows_of(i)], go_send.at[g], relay_recv.at[g], (section, 1)).start()

            return carry

        lax.fori_loop(max(low, 1), high, go, 0)

    stay = pltpu.make_async_copy(send.at[rows_of(mine)], recv.at[rows_of(0)], self_sem)
    stay.start()

    @pl.when(section > 0)
    def _():
        def tell(i, carry):
            target = device(*peer(i, 1), section - 1)

            @pl.when(jnp.logical_not((section == 1) & (target[1] == 0)))
            def _():
                pl.semaphore_signal(ready, inc=1, device_id=target, device_id_type=MESH)

            return carry

        lax.fori_loop(0, before_count, tell, 0)

    launch(sibling_copies, jnp.logical_not(sibling_late))
    inputs[3].wait()
    far_copies = [
        remote(src, dst, far_send.at[j], far_recv.at[j], following)
        for j, (src, dst) in enumerate(
            (
                (routes_ref, routes_far),
                (gates_ref, gates_far),
                (x_ref.at[:, pl.ds(begin, UNITS * UNIT)], x_far),
            )
        )
    ]

    fill_mix(mix, is0, is1, gates_ref[...])

    @pl.when(punctual & (section < last))
    def _():
        pl.semaphore_wait(ready, onward_count)

    @pl.when(passed < UNITS)
    def _():
        for copy in far_copies:
            copy.start()

    @pl.when(near_late)
    def _():
        pl.semaphore_wait(late_ready, 1)

    launch(beside_copies, beside_late)
    launch(sibling_copies, sibling_late)

    forward_copies = [
        remote(
            dst.at[pl.ds(2 * quarter, quarter)], dst.at[pl.ds(3 * quarter, quarter)],
            fwd_send.at[j], fwd_recv.at[j], sibling,
        )
        for j, (_, dst) in enumerate(weights)
    ]
    for copy in own:
        copy.wait()
    for copy in sibling_copies:
        copy.wait()
    stay.wait()

    def went(g):
        rows = group_rows(g, 1 if g == 0 else 0)
        return remote(send.at[rows], recv.at[rows], go_send.at[g], go_recv.at[g], sibling)

    def home_copy(c, g):
        rows = group_rows(g, 1 if g == 0 else 0)
        return remote(res[c].at[rows], back[c].at[rows], home_send.at[c, g], home_recv.at[c, g], sibling)

    def keep(c):
        return pltpu.make_async_copy(res[c].at[rows_of(0)], back[c].at[rows_of(mine)], home_self.at[c])

    def passing(g):
        rows = group_rows(g, 1 if g == 0 else 0)
        return remote(relay.at[rows], recv.at[rows], relay_send.at[g], go_recv.at[g], sibling)

    def came_to_pass(g):
        rows = group_rows(g, 1 if g == 0 else 0)
        return remote(send.at[rows], relay.at[rows], go_send.at[g], relay_recv.at[g], sibling)

    for j in range(2):
        with jax.named_scope(f"p_beside{j}"):
            beside_copies[j].wait_recv()
            forward_copies[j].start()
    units = 256
    for g, (low, high) in enumerate(GROUPS):
        rows = group_rows(g)
        with jax.named_scope("p_arrive"):
            went(g).wait_recv()

        @pl.when(sibling_late)
        def _(g=g):
            came_to_pass(g).wait_recv()
            passing(g).start()

        if g == 0:
            with jax.named_scope("p_fwd0"):
                forward_copies[0].wait_recv()

        def up(i, carry, rows=rows):
            part = pl.ds(pl.multiple_of(i * units, units), units)
            v = lax.dot_general(
                recv[rows, :], up_all[part, :], (((1,), (1,)), ((), ())),
                preferred_element_type=jnp.float32,
            )
            inner = 0.7978845608028654 * (v + 0.044715 * (v * v * v))
            hidden[rows, part] = (0.5 * v * (1.0 + jnp.tanh(inner))).astype(jnp.bfloat16)
            return carry

        with jax.named_scope("p_up"):
            lax.fori_loop(0, 4 * quarter // units, up, 0)
        if g == 0:
            with jax.named_scope("p_fwd1"):
                forward_copies[1].wait_recv()
        for c in range(chunks):
            with jax.named_scope("p_down"):
                res[c][rows, :] = jnp.dot(
                    hidden[rows, :], down_all[:, pl.ds(STARTS[c], WIDTHS[c])],
                    preferred_element_type=jnp.float32,
                ).astype(jnp.bfloat16)

            def home(i, carry, c=c, g=g):
                py, px = peer(i, -1)
                remote(
                    res[c].at[rows_of(i)], back[c].at[rows_of(mine)],
                    home_send.at[c, g], home_recv.at[c, g], device(py, px),
                ).start()
                return carry

            with jax.named_scope("p_home"):
                lax.fori_loop(max(low, 1), high, home, 0)
            if g == 0:
                keep(c).start()
        tail = jnp.dot(
            hidden[rows, :], down_all[:, pl.ds(begin, UNITS * UNIT)], preferred_element_type=jnp.float32
        ).astype(jnp.bfloat16)
        for j in range(UNITS):
            res_unit[j, rows, :] = tail[:, j * UNIT : (j + 1) * UNIT]

    def unit_wait(d, j, g):
        rows = group_rows(g, 1 if g == 0 else 0)
        return remote(
            res_unit.at[j, rows], back_unit.at[d, j, rows],
            unit_send.at[j, g], unit_recv.at[d, j, g], sibling,
        )

    def unit_keep(j):
        return pltpu.make_async_copy(
            res_unit.at[j, rows_of(0)], back_unit.at[0, j, rows_of(mine)], unit_self.at[j]
        )

    def unit_hand(j):
        return remote(
            res_unit.at[j, rows_of(0)], back_unit.at[1, j, rows_of(mine)],
            unit_near.at[j], unit_far.at[j], following,
        )

    def unit_columns(j):
        return pl.ds(pl.multiple_of(begin + j * UNIT, UNIT), UNIT)

    def unit_onward(j):
        return remote(
            out_unit.at[j], out_ref.at[:, unit_columns(j)],
            unit_out_send.at[j], unit_out_recv.at[j], following,
        )

    def unit_store(j):
        return pltpu.make_async_copy(out_unit.at[UNITS + j], out_ref.at[:, unit_columns(j)], far_out.at[j])

    def unit_home(j, carry):
        d = (j >= passed).astype(jnp.int32)
        where = lax.rem(section + d, sections)
        for g, (low, high) in enumerate(GROUPS):

            def home(i, inner, g=g):
                py, px = peer(i, -1)
                remote(
                    res_unit.at[j, rows_of(i)], back_unit.at[d, j, rows_of(mine)],
                    unit_send.at[j, g], unit_recv.at[d, j, g], device(py, px, where),
                ).start()
                return inner

            lax.fori_loop(max(low, 1), high, home, 0)

        @pl.when(j < passed)
        def _():
            unit_keep(j).start()

        @pl.when(j >= passed)
        def _():
            unit_hand(j).start()

        return carry

    with jax.named_scope("p_unithome"):
        lax.fori_loop(0, UNITS, unit_home, 0)

    onward = [
        remote(
            outb[c], out_ref.at[:, pl.ds(STARTS[c], WIDTHS[c])], out_send.at[c], out_recv.at[c], following
        )
        for c in range(chunks)
    ]
    for c in range(chunks):
        with jax.named_scope("p_came"):
            keep(c).wait()
            for g in range(len(GROUPS)):
                home_copy(c, g).wait_recv()
        with jax.named_scope("p_mix"):
            part = pl.ds(STARTS[c], WIDTHS[c])
            total = x_ref[:, part].astype(jnp.float32) + mixed(mix, back[c][...])
            outb[c][...] = total.astype(jnp.bfloat16)
            onward[c].start()

    def unit_finish(j, carry):
        unit_keep(j).wait()
        for g in range(len(GROUPS)):
            unit_wait(0, j, g).wait_recv()
        total = x_ref[:, unit_columns(j)].astype(jnp.float32) + mixed(mix, back_unit[0, j])
        out_unit[j] = total.astype(jnp.bfloat16)
        unit_onward(j).start()
        return carry

    def unit_finish_far(j, carry):
        unit_hand(j).wait_recv()
        for g in range(len(GROUPS)):
            unit_wait(1, j, g).wait_recv()
        part = pl.ds(pl.multiple_of(j * UNIT, UNIT), UNIT)
        total = x_far[:, part].astype(jnp.float32) + mixed(mix_far, back_unit[1, j])
        out_unit[UNITS + j] = total.astype(jnp.bfloat16)
        unit_store(j).start()
        return carry

    with jax.named_scope("p_unitfin"):
        lax.fori_loop(0, passed, unit_finish, 0)
    @pl.when(taken < UNITS)
    def _():
        for copy in far_copies:
            copy.wait_recv()
        fill_mix(mix_far, *places(routes_far[...]), gates_far[...])

    with jax.named_scope("p_unitfar"):
        lax.fori_loop(taken, UNITS, unit_finish_far, 0)

    for j in range(2):
        beside_copies[j].wait_send()
        forward_copies[j].wait_send()
    with jax.named_scope("p_drain"):
        for g in range(len(GROUPS)):
            went(g).wait_send()

            @pl.when(sibling_late)
            def _(g=g):
                passing(g).wait_send()

            for c in range(chunks):
                home_copy(c, g).wait_send()
        for c in range(chunks):
            onward[c].wait()

        def drain_sent(j, carry):
            for g in range(len(GROUPS)):
                unit_wait(0, j, g).wait_send()
            return carry

        def drain_onward(j, carry):
            unit_onward(j).wait_send()
            return carry

        def drain_hand(j, carry):
            unit_hand(j).wait_send()
            return carry

        def drain_came(j, carry):
            unit_onward(j).wait_recv()
            return carry

        def drain_store(j, carry):
            unit_store(j).wait()
            return carry

        lax.fori_loop(0, UNITS, drain_sent, 0)
        lax.fori_loop(0, passed, drain_onward, 0)
        lax.fori_loop(passed, UNITS, drain_hand, 0)
        lax.fori_loop(0, taken, drain_came, 0)
        lax.fori_loop(taken, UNITS, drain_store, 0)

        @pl.when(passed < UNITS)
        def _():
            for copy in far_copies:
                copy.wait_send()


def shards(carried, norm_gain, w_up, w_down, routes, gate_weights):
    tokens, width = carried.shape[1:]
    quarter = w_down.shape[1]
    slots = EXPERTS * 32
    bf16 = jnp.bfloat16
    dma = pltpu.SemaphoreType.DMA
    whole = pl.BlockSpec(memory_space=pl.ANY)
    chunks = len(WIDTHS)
    out = pl.pallas_call(
        kernel,
        name="section_layer",
        out_shape=jax.ShapeDtypeStruct((tokens, width), bf16),
        in_specs=[whole] * 6,
        out_specs=whole,
        scratch_shapes=[
            pltpu.VMEM((tokens, width), bf16),
            pltpu.VMEM((1, width), jnp.float32),
            pltpu.VMEM((2, tokens), jnp.int32),
            pltpu.VMEM((2, tokens), jnp.float32),
            pltpu.VMEM((4 * quarter, width), bf16),
            pltpu.VMEM((4 * quarter, width), bf16),
            pltpu.VMEM((tokens, width), bf16),
            pltpu.VMEM((slots, width), bf16),
            pltpu.VMEM((slots, width), bf16),
            pltpu.VMEM((slots, 4 * quarter), bf16),
            pltpu.VMEM((tokens, 2 * slots), bf16),
            pltpu.VMEM((tokens, UNITS * UNIT), bf16),
            pltpu.VMEM((2, tokens), jnp.int32),
            pltpu.VMEM((2, tokens), jnp.float32),
            pltpu.VMEM((tokens, 2 * slots), bf16),
            pltpu.VMEM((UNITS, slots, UNIT), bf16),
            pltpu.VMEM((2, UNITS, slots, UNIT), bf16),
            pltpu.VMEM((2 * UNITS, tokens, UNIT), bf16),
            pltpu.VMEM((slots, width), bf16),
            *[pltpu.VMEM((slots, w), bf16) for w in WIDTHS],
            *[pltpu.VMEM((slots, w), bf16) for w in WIDTHS],
            *[pltpu.VMEM((tokens, w), bf16) for w in WIDTHS],
            dma((4,)), dma((2,)), dma((2,)), dma((2,)), dma((2,)), dma((2,)), dma((2,)), dma((2,)),
            dma, dma((len(GROUPS),)), dma((len(GROUPS),)),
            dma((chunks,)), dma((chunks, len(GROUPS))), dma((chunks, len(GROUPS))),
            dma((chunks,)), dma((chunks,)),
            dma((3,)), dma((3,)), dma((UNITS,)), dma((UNITS, len(GROUPS))), dma((2, UNITS, len(GROUPS))),
            dma((UNITS,)), dma((UNITS,)), dma((UNITS,)), dma((UNITS,)), dma((UNITS,)),
            pltpu.SemaphoreType.REGULAR, pltpu.SemaphoreType.REGULAR, dma((len(GROUPS),)), dma((len(GROUPS),)),
        ],
        compiler_params=pltpu.CompilerParams(
            collective_id=0, has_side_effects=True, vmem_limit_bytes=56 * 1024 * 1024
        ),
        cost_estimate=pl.CostEstimate(
            flops=16 * slots * width * quarter, bytes_accessed=8 * quarter * width, transcendentals=0
        ),
    )(carried[0], norm_gain, w_up[0].T, w_down[0], routes[0, 0].T, gate_weights[0, 0].T)
    return out[None]


def solution(mesh):
    in_specs = (
        P("section", "expert", None),
        P("section", None),
        P("section", None, "expert"),
        P("section", "expert", None),
        P(None, "section", "expert", None),
        P(None, "section", "expert", None),
    )
    return jax.shard_map(
        shards, mesh=mesh, in_specs=in_specs, out_specs=P("section", "expert", None), check_vma=False
    )
```

```python
import jax
import jax.numpy as jnp
from jax import lax
from jax.experimental import pallas as pl
from jax.experimental.pallas import tpu as pltpu
from jax.sharding import PartitionSpec as P

MESH = pl.DeviceIdType.MESH
NX, NY, NC = 4, 8, 2
PEERS = 2 * NY
EXPERTS = NX * NY // 2
GROUPS = ((0, 8), (8, 16))
WIDTHS = (384, 384, 256, 256, 128)
UNITS, UNIT = 5, 128
DIRECT = 6
STARTS = tuple(sum(WIDTHS[:c]) for c in range(len(WIDTHS)))


def kernel(
    x_hbm, gain_hbm, up_ref, down_ref, routes_hbm, gates_hbm, out_ref,
    x_ref, gain_ref, routes_ref, gates_ref,
    up_all, down_all, normed, send, recv, hidden, mix,
    x_far, routes_far, gates_far, mix_far, res_unit, back_unit, out_unit, relay, *rest,
):
    chunks = len(WIDTHS)
    res, back, outb = rest[:chunks], rest[chunks : 2 * chunks], rest[2 * chunks : 3 * chunks]
    (
        in_sem, own_sem, sib_send, sib_recv, xp_send, xp_recv, fwd_send, fwd_recv,
        self_sem, go_send, go_recv, home_self, home_send, home_recv, out_send, out_recv,
        far_send, far_recv, unit_self, unit_send, unit_recv, unit_near, unit_far, unit_out_send, unit_out_recv, far_out, ready, late_ready, relay_send, relay_recv,
    ) = rest[3 * chunks :]
    tokens, width = x_ref.shape
    quarter = up_ref.shape[0]
    slots = send.shape[0]
    cap = slots // EXPERTS
    sections = lax.axis_size("section")
    section = lax.axis_index("section")
    me = lax.axis_index("expert")
    core = lax.rem(me, NC)
    chip = lax.div(me, NC)
    x = lax.rem(chip, NX)
    y = lax.div(chip, NX)
    mine = y * 2 + lax.div(x, 2)

    def peer(i, sign):
        k = lax.div(i, 2)
        half = lax.div(k + 1, 2)
        dy = half * (2 * lax.rem(k, 2) - 1)
        return lax.rem(y + NY + sign * dy, NY), lax.rem(i, 2) * (NX - 1 - 2 * x) + x

    def device(py, px, where=section):
        return (where, (py * NX + px) * NC + core)

    sibling = (section, chip * NC + 1 - core)
    beside = (section, (chip + 1 - 2 * lax.rem(x, 2)) * NC + core)
    following = (lax.rem(section + 1, sections), me)
    previous = (lax.rem(section + sections - 1, sections), me)
    begin = STARTS[-1] + WIDTHS[-1]
    passed = UNITS - lax.min(UNITS, lax.max(0, DIRECT - lax.rem(section + 1, sections)))
    taken = UNITS - lax.min(UNITS, lax.max(0, DIRECT - section))

    last = sections - 1
    kin = (core == 0) & ((x == 0) | (x == NX - 1))
    is_late = (section == 0) & (me == 0)
    sibling_late = (section == 0) & (me == 1)
    beside_late = (section == 0) & (me == NC)
    near_late = (section == 0) & (me != 0) & (kin | (me == 1) | (me == NC))
    next_late = (section == 1) & jnp.where(taken < UNITS, kin, me == 0)
    punctual = jnp.logical_not(is_late)
    onward_count = jnp.where(passed < UNITS, PEERS, 1)
    before_count = jnp.where(taken < UNITS, PEERS, 1)

    def hello(target):
        pl.semaphore_signal(barrier, inc=1, device_id=target, device_id_type=MESH)

    barrier = pltpu.get_barrier_semaphore()
    inputs = [
        pltpu.make_async_copy(src, dst, in_sem.at[j])
        for j, (src, dst) in enumerate(
            ((routes_hbm, routes_ref), (gain_hbm, gain_ref), (x_hbm, x_ref), (gates_hbm, gates_ref))
        )
    ]
    for copy in inputs:
        copy.start()

    def greet(i, carry):
        hello(device(*peer(PEERS - i, -1)))
        return carry

    def greet_at(where, number):
        def greet_far(i, carry):
            hello(device(*peer(i, -1), where))
            return carry

        lax.fori_loop(0, number, greet_far, 0)

    @pl.when(punctual)
    def _():
        lax.fori_loop(1, PEERS, greet, 0)
        hello(sibling)
        hello(beside)

    @pl.when(punctual & (section < last))
    def _():
        greet_at(section + 1, onward_count)

    @pl.when(section == 0)
    def _():
        greet_at(last, before_count)

    @pl.when(next_late)
    def _():
        hello((0, 0))

    @pl.when(sibling_late)
    def _():
        def greet_for(i, carry):
            py, px = peer(i, -1)
            hello((section, (py * NX + px) * NC))
            return carry

        lax.fori_loop(1, PEERS, greet_for, 0)

    own = [
        pltpu.make_async_copy(src, dst.at[pl.ds(0, quarter)], own_sem.at[j])
        for j, (src, dst) in enumerate(((up_ref, up_all), (down_ref, down_all)))
    ]
    for copy in own:
        copy.start()

    def places(ids):
        names = lax.broadcasted_iota(jnp.int32, (EXPERTS, tokens), 0)
        first = (names == ids[0:1, :]).astype(jnp.float32)
        second = (names == ids[1:2, :]).astype(jnp.float32)
        earlier = (
            lax.broadcasted_iota(jnp.int32, (tokens, tokens), 0)
            < lax.broadcasted_iota(jnp.int32, (tokens, tokens), 1)
        ).astype(jnp.bfloat16)
        count = jnp.dot(
            (first + second).astype(jnp.bfloat16), earlier, preferred_element_type=jnp.float32
        )
        place0 = jnp.sum(count * first, axis=0, keepdims=True).astype(jnp.int32) + ids[0:1, :] * cap
        place1 = jnp.sum(count * second, axis=0, keepdims=True).astype(jnp.int32) + ids[1:2, :] * cap
        slot = lax.broadcasted_iota(jnp.int32, (slots, tokens), 0)
        return slot == place0, slot == place1

    def fill_mix(mix, is0, is1, gates):
        weight = jnp.where(is0, gates[0:1, :], 0.0) + jnp.where(is1, gates[1:2, :], 0.0)
        weight = weight.T
        high_part = weight.astype(jnp.bfloat16)
        mix[:, pl.ds(0, slots)] = high_part
        mix[:, pl.ds(slots, slots)] = (weight - high_part.astype(jnp.float32)).astype(jnp.bfloat16)

    def mixed(mix, rows):
        total = jnp.dot(mix[:, pl.ds(0, slots)], rows, preferred_element_type=jnp.float32)
        return total + jnp.dot(mix[:, pl.ds(slots, slots)], rows, preferred_element_type=jnp.float32)

    inputs[0].wait()
    is0, is1 = places(routes_ref[...])
    assign = (is0 | is1).astype(jnp.float32).astype(jnp.bfloat16)

    block = 48

    def norm(i, carry):
        rows = pl.ds(pl.multiple_of(i * block, 16), block)
        values = x_ref[rows, :].astype(jnp.float32)
        inverse = lax.rsqrt(jnp.mean(values * values, axis=-1, keepdims=True) + 1e-05)
        normed[rows, :] = (values * inverse * gain_ref[...]).astype(jnp.bfloat16)
        return carry

    inputs[1].wait()
    inputs[2].wait()
    with jax.named_scope("p_norm"):
        lax.fori_loop(0, tokens // block, norm, 0)

    piece = 512

    def fill(i, carry):
        part = pl.ds(pl.multiple_of(i * piece, piece), piece)
        send[:, part] = jnp.dot(
            assign, normed[:, part], preferred_element_type=jnp.float32
        ).astype(jnp.bfloat16)
        return carry

    with jax.named_scope("p_fill"):
        lax.fori_loop(0, width // piece, fill, 0)

    with jax.named_scope("p_barrier"):
        pl.semaphore_wait(
            barrier,
            PEERS + 1
            - (sibling_late | beside_late).astype(jnp.int32)
            + jnp.where(section > 0, before_count, 0)
            - next_late.astype(jnp.int32)
            + jnp.where((section == last) | is_late, onward_count, 0),
        )

    def remote(src, dst, send_sem, recv_sem, target):
        return pltpu.make_async_remote_copy(
            src_ref=src, dst_ref=dst, send_sem=send_sem, recv_sem=recv_sem,
            device_id=target, device_id_type=MESH,
        )

    def rows_of(which):
        return pl.ds(pl.multiple_of(which * cap, cap), cap)

    def group_rows(g, skip=0):
        low, high = GROUPS[g]
        return pl.ds((low + skip) * cap, (high - low - skip) * cap)

    weights = ((up_ref, up_all), (down_ref, down_all))
    beside_copies = [
        remote(src, dst.at[pl.ds(2 * quarter, quarter)], xp_send.at[j], xp_recv.at[j], beside)
        for j, (src, dst) in enumerate(weights)
    ]
    sibling_copies = [
        remote(src, dst.at[pl.ds(quarter, quarter)], sib_send.at[j], sib_recv.at[j], sibling)
        for j, (src, dst) in enumerate(weights)
    ]
    @pl.when(is_late)
    def _():
        def arrived(target):
            pl.semaphore_signal(late_ready, inc=1, device_id=target, device_id_type=MESH)

        def tell_peer(i, carry):
            arrived(device(*peer(i, 1)))
            return carry

        lax.fori_loop(1, PEERS, tell_peer, 0)
        arrived(sibling)
        arrived(beside)

    def launch(copies, here):
        @pl.when(here)
        def _():
            for copy in copies:
                copy.start()

    launch(beside_copies, jnp.logical_not(beside_late))
    for g, (low, high) in enumerate(GROUPS):

        def go(i, carry, g=g):
            py, px = peer(i, 1)
            target = device(py, px)
            source = send.at[rows_of(py * 2 + lax.div(px, 2))]
            to_late = (section == 0) & (target[1] == 0)

            @pl.when(jnp.logical_not(to_late))
            def _():
                remote(source, recv.at[rows_of(i)], go_send.at[g], go_recv.at[g], target).start()

            @pl.when(to_late)
            def _():
                remote(source, relay.at[rows_of(i)], go_send.at[g], relay_recv.at[g], (section, 1)).start()

            return carry

        lax.fori_loop(max(low, 1), high, go, 0)

    stay = pltpu.make_async_copy(send.at[rows_of(mine)], recv.at[rows_of(0)], self_sem)
    stay.start()

    @pl.when(section > 0)
    def _():
        def tell(i, carry):
            target = device(*peer(i, 1), section - 1)

            @pl.when(jnp.logical_not((section == 1) & (target[1] == 0)))
            def _():
                pl.semaphore_signal(ready, inc=1, device_id=target, device_id_type=MESH)

            return carry

        lax.fori_loop(0, before_count, tell, 0)

    launch(sibling_copies, jnp.logical_not(sibling_late))
    inputs[3].wait()
    far_copies = [
        remote(src, dst, far_send.at[j], far_recv.at[j], following)
        for j, (src, dst) in enumerate(
            (
                (routes_ref, routes_far),
                (gates_ref, gates_far),
                (x_ref.at[:, pl.ds(begin, UNITS * UNIT)], x_far),
            )
        )
    ]

    fill_mix(mix, is0, is1, gates_ref[...])

    @pl.when(punctual & (section < last))
    def _():
        pl.semaphore_wait(ready, onward_count)

    @pl.when(passed < UNITS)
    def _():
        for copy in far_copies:
            copy.start()

    @pl.when(near_late)
    def _():
        pl.semaphore_wait(late_ready, 1)

    launch(beside_copies, beside_late)
    launch(sibling_copies, sibling_late)

    forward_copies = [
        remote(
            dst.at[pl.ds(2 * quarter, quarter)], dst.at[pl.ds(3 * quarter, quarter)],
            fwd_send.at[j], fwd_recv.at[j], sibling,
        )
        for j, (_, dst) in enumerate(weights)
    ]
    for copy in own:
        copy.wait()
    for copy in sibling_copies:
        copy.wait()
    stay.wait()

    def went(g):
        rows = group_rows(g, 1 if g == 0 else 0)
        return remote(send.at[rows], recv.at[rows], go_send.at[g], go_recv.at[g], sibling)

    def home_copy(c, g):
        rows = group_rows(g, 1 if g == 0 else 0)
        return remote(res[c].at[rows], back[c].at[rows], home_send.at[c, g], home_recv.at[c, g], sibling)

    def keep(c):
        return pltpu.make_async_copy(res[c].at[rows_of(0)], back[c].at[rows_of(mine)], home_self.at[c])

    def passing(g):
        rows = group_rows(g, 1 if g == 0 else 0)
        return remote(relay.at[rows], recv.at[rows], relay_send.at[g], go_recv.at[g], sibling)

    def came_to_pass(g):
        rows = group_rows(g, 1 if g == 0 else 0)
        return remote(send.at[rows], relay.at[rows], go_send.at[g], relay_recv.at[g], sibling)

    for j in range(2):
        with jax.named_scope(f"p_beside{j}"):
            beside_copies[j].wait_recv()
            forward_copies[j].start()
    units = 256
    for g, (low, high) in enumerate(GROUPS):
        rows = group_rows(g)
        with jax.named_scope("p_arrive"):
            went(g).wait_recv()

        @pl.when(sibling_late)
        def _(g=g):
            came_to_pass(g).wait_recv()
            passing(g).start()

        if g == 0:
            with jax.named_scope("p_fwd0"):
                forward_copies[0].wait_recv()

        def up(i, carry, rows=rows):
            part = pl.ds(pl.multiple_of(i * units, units), units)
            v = lax.dot_general(
                recv[rows, :], up_all[part, :], (((1,), (1,)), ((), ())),
                preferred_element_type=jnp.float32,
            )
            inner = 0.7978845608028654 * (v + 0.044715 * (v * v * v))
            hidden[rows, part] = (0.5 * v * (1.0 + jnp.tanh(inner))).astype(jnp.bfloat16)
            return carry

        with jax.named_scope("p_up"):
            lax.fori_loop(0, 4 * quarter // units, up, 0)
        if g == 0:
            with jax.named_scope("p_fwd1"):
                forward_copies[1].wait_recv()
        for c in range(chunks):
            with jax.named_scope("p_down"):
                res[c][rows, :] = jnp.dot(
                    hidden[rows, :], down_all[:, pl.ds(STARTS[c], WIDTHS[c])],
                    preferred_element_type=jnp.float32,
                ).astype(jnp.bfloat16)

            def home(i, carry, c=c, g=g):
                py, px = peer(i, -1)
                remote(
                    res[c].at[rows_of(i)], back[c].at[rows_of(mine)],
                    home_send.at[c, g], home_recv.at[c, g], device(py, px),
                ).start()
                return carry

            with jax.named_scope("p_home"):
                lax.fori_loop(max(low, 1), high, home, 0)
            if g == 0:
                keep(c).start()
        tail = jnp.dot(
            hidden[rows, :], down_all[:, pl.ds(begin, UNITS * UNIT)], preferred_element_type=jnp.float32
        ).astype(jnp.bfloat16)
        for j in range(UNITS):
            res_unit[j, rows, :] = tail[:, j * UNIT : (j + 1) * UNIT]

    def unit_wait(d, j, g):
        rows = group_rows(g, 1 if g == 0 else 0)
        return remote(
            res_unit.at[j, rows], back_unit.at[d, j, rows],
            unit_send.at[j, g], unit_recv.at[d, j, g], sibling,
        )

    def unit_keep(j):
        return pltpu.make_async_copy(
            res_unit.at[j, rows_of(0)], back_unit.at[0, j, rows_of(mine)], unit_self.at[j]
        )

    def unit_hand(j):
        return remote(
            res_unit.at[j, rows_of(0)], back_unit.at[1, j, rows_of(mine)],
            unit_near.at[j], unit_far.at[j], following,
        )

    def unit_columns(j):
        return pl.ds(pl.multiple_of(begin + j * UNIT, UNIT), UNIT)

    def unit_onward(j):
        return remote(
            out_unit.at[j], out_ref.at[:, unit_columns(j)],
            unit_out_send.at[j], unit_out_recv.at[j], following,
        )

    def unit_store(j):
        return pltpu.make_async_copy(out_unit.at[UNITS + j], out_ref.at[:, unit_columns(j)], far_out.at[j])

    def unit_home(j, carry):
        d = (j >= passed).astype(jnp.int32)
        where = lax.rem(section + d, sections)
        for g, (low, high) in enumerate(GROUPS):

            def home(i, inner, g=g):
                py, px = peer(i, -1)
                remote(
                    res_unit.at[j, rows_of(i)], back_unit.at[d, j, rows_of(mine)],
                    unit_send.at[j, g], unit_recv.at[d, j, g], device(py, px, where),
                ).start()
                return inner

            lax.fori_loop(max(low, 1), high, home, 0)

        @pl.when(j < passed)
        def _():
            unit_keep(j).start()

        @pl.when(j >= passed)
        def _():
            unit_hand(j).start()

        return carry

    with jax.named_scope("p_unithome"):
        lax.fori_loop(0, UNITS, unit_home, 0)

    onward = [
        remote(
            outb[c], out_ref.at[:, pl.ds(STARTS[c], WIDTHS[c])], out_send.at[c], out_recv.at[c], following
        )
        for c in range(chunks)
    ]
    for c in range(chunks):
        with jax.named_scope("p_came"):
            keep(c).wait()
            for g in range(len(GROUPS)):
                home_copy(c, g).wait_recv()
        with jax.named_scope("p_mix"):
            part = pl.ds(STARTS[c], WIDTHS[c])
            total = x_ref[:, part].astype(jnp.float32) + mixed(mix, back[c][...])
            outb[c][...] = total.astype(jnp.bfloat16)
            onward[c].start()

    def unit_finish(j, carry):
        unit_keep(j).wait()
        for g in range(len(GROUPS)):
            unit_wait(0, j, g).wait_recv()
        total = x_ref[:, unit_columns(j)].astype(jnp.float32) + mixed(mix, back_unit[0, j])
        out_unit[j] = total.astype(jnp.bfloat16)
        unit_onward(j).start()
        return carry

    def unit_finish_far(j, carry):
        unit_hand(j).wait_recv()
        for g in range(len(GROUPS)):
            unit_wait(1, j, g).wait_recv()
        part = pl.ds(pl.multiple_of(j * UNIT, UNIT), UNIT)
        total = x_far[:, part].astype(jnp.float32) + mixed(mix_far, back_unit[1, j])
        out_unit[UNITS + j] = total.astype(jnp.bfloat16)
        unit_store(j).start()
        return carry

    with jax.named_scope("p_unitfin"):
        lax.fori_loop(0, passed, unit_finish, 0)
    @pl.when(taken < UNITS)
    def _():
        for copy in far_copies:
            copy.wait_recv()
        fill_mix(mix_far, *places(routes_far[...]), gates_far[...])

    with jax.named_scope("p_unitfar"):
        lax.fori_loop(taken, UNITS, unit_finish_far, 0)

    for j in range(2):
        beside_copies[j].wait_send()
        forward_copies[j].wait_send()
    with jax.named_scope("p_drain"):
        for g in range(len(GROUPS)):
            went(g).wait_send()

            @pl.when(sibling_late)
            def _(g=g):
                passing(g).wait_send()

            for c in range(chunks):
                home_copy(c, g).wait_send()
        for c in range(chunks):
            onward[c].wait()

        def drain_sent(j, carry):
            for g in range(len(GROUPS)):
                unit_wait(0, j, g).wait_send()
            return carry

        def drain_onward(j, carry):
            unit_onward(j).wait_send()
            return carry

        def drain_hand(j, carry):
            unit_hand(j).wait_send()
            return carry

        def drain_came(j, carry):
            unit_onward(j).wait_recv()
            return carry

        def drain_store(j, carry):
            unit_store(j).wait()
            return carry

        lax.fori_loop(0, UNITS, drain_sent, 0)
        lax.fori_loop(0, passed, drain_onward, 0)
        lax.fori_loop(passed, UNITS, drain_hand, 0)
        lax.fori_loop(0, taken, drain_came, 0)
        lax.fori_loop(taken, UNITS, drain_store, 0)

        @pl.when(passed < UNITS)
        def _():
            for copy in far_copies:
                copy.wait_send()


def shards(carried, norm_gain, w_up, w_down, routes, gate_weights):
    tokens, width = carried.shape[1:]
    quarter = w_down.shape[1]
    slots = EXPERTS * 32
    bf16 = jnp.bfloat16
    dma = pltpu.SemaphoreType.DMA
    whole = pl.BlockSpec(memory_space=pl.ANY)
    chunks = len(WIDTHS)
    out = pl.pallas_call(
        kernel,
        name="section_layer",
        out_shape=jax.ShapeDtypeStruct((tokens, width), bf16),
        in_specs=[whole] * 6,
        out_specs=whole,
        scratch_shapes=[
            pltpu.VMEM((tokens, width), bf16),
            pltpu.VMEM((1, width), jnp.float32),
            pltpu.VMEM((2, tokens), jnp.int32),
            pltpu.VMEM((2, tokens), jnp.float32),
            pltpu.VMEM((4 * quarter, width), bf16),
            pltpu.VMEM((4 * quarter, width), bf16),
            pltpu.VMEM((tokens, width), bf16),
            pltpu.VMEM((slots, width), bf16),
            pltpu.VMEM((slots, width), bf16),
            pltpu.VMEM((slots, 4 * quarter), bf16),
            pltpu.VMEM((tokens, 2 * slots), bf16),
            pltpu.VMEM((tokens, UNITS * UNIT), bf16),
            pltpu.VMEM((2, tokens), jnp.int32),
            pltpu.VMEM((2, tokens), jnp.float32),
            pltpu.VMEM((tokens, 2 * slots), bf16),
            pltpu.VMEM((UNITS, slots, UNIT), bf16),
            pltpu.VMEM((2, UNITS, slots, UNIT), bf16),
            pltpu.VMEM((2 * UNITS, tokens, UNIT), bf16),
            pltpu.VMEM((slots, width), bf16),
            *[pltpu.VMEM((slots, w), bf16) for w in WIDTHS],
            *[pltpu.VMEM((slots, w), bf16) for w in WIDTHS],
            *[pltpu.VMEM((tokens, w), bf16) for w in WIDTHS],
            dma((4,)), dma((2,)), dma((2,)), dma((2,)), dma((2,)), dma((2,)), dma((2,)), dma((2,)),
            dma, dma((len(GROUPS),)), dma((len(GROUPS),)),
            dma((chunks,)), dma((chunks, len(GROUPS))), dma((chunks, len(GROUPS))),
            dma((chunks,)), dma((chunks,)),
            dma((3,)), dma((3,)), dma((UNITS,)), dma((UNITS, len(GROUPS))), dma((2, UNITS, len(GROUPS))),
            dma((UNITS,)), dma((UNITS,)), dma((UNITS,)), dma((UNITS,)), dma((UNITS,)),
            pltpu.SemaphoreType.REGULAR, pltpu.SemaphoreType.REGULAR, dma((len(GROUPS),)), dma((len(GROUPS),)),
        ],
        compiler_params=pltpu.CompilerParams(
            collective_id=0, has_side_effects=True, vmem_limit_bytes=56 * 1024 * 1024
        ),
        cost_estimate=pl.CostEstimate(
            flops=16 * slots * width * quarter, bytes_accessed=8 * quarter * width, transcendentals=0
        ),
    )(carried[0], norm_gain, w_up[0].T, w_down[0], routes[0, 0].T, gate_weights[0, 0].T)
    return out[None]


def solution(mesh):
    in_specs = (
        P("section", "expert", None),
        P("section", None),
        P("section", None, "expert"),
        P("section", "expert", None),
        P(None, "section", "expert", None),
        P(None, "section", "expert", None),
    )
    return jax.shard_map(
        shards, mesh=mesh, in_specs=in_specs, out_specs=P("section", "expert", None), check_vma=False
    )
```
